32 devices in a mesh: pipe: 2 (over core), expert: 4 (over z), dp: 4 (over y, x).
Axes of the slice: x: 2, y: 2, z: 4, core: 2. Of those that a mesh axis runs over, the one named last changes fastest.
Arguments:
- tokens: bfloat16 [2, 128, 3584], P('pipe', ('expert', 'dp')), may hold values from -6 to 6
- grad_out: bfloat16 [2, 128, 3584], P('pipe', ('expert', 'dp')), may hold values from -1.5 to 1.5
- routes: int32 [2, 128, 1], P('pipe', ('expert', 'dp')), may hold values from 0 to 1; in each aligned block of 8 rows (0 to 7, 8 to 15, ..., all dimensions but the last counted through in order) at most 6 rows name the same one
- combine: bfloat16 [2, 128, 1], P('pipe', ('expert', 'dp')), may hold values from 0.25 to 2.5
- w_gate: bfloat16 [2, 3584, 512], P('pipe', 'dp', 'expert'), may hold values from -0.09375 to 0.09375
- w_up: bfloat16 [2, 3584, 512], P('pipe', 'dp', 'expert'), may hold values from -0.09375 to 0.09375
- w_down: bfloat16 [2, 3584, 512], P('pipe', 'dp', 'expert'), may hold values from -0.375 to 0.375
Outputs:
- passed: bfloat16 [2, 128, 3584], P('pipe', ('expert', 'dp'))
- grad_combine: float32 [2, 128, 1], P('pipe', ('expert', 'dp'))
- grad_gate: float32 [2, 3584, 512], P('pipe', 'dp', 'expert')
- grad_up: float32 [2, 3584, 512], P('pipe', 'dp', 'expert')
- grad_down: float32 [2, 3584, 512], P('pipe', 'dp', 'expert')
The draws below stay inside these ranges and needn't reach their ends.
Inputs may be any that keep to these rules, and one draw needn't show every extreme that they name: `routes`: each token names 1 different experts; among the 8 tokens of one device no expert is named more than 6 times, and in some device's tokens an expert is named exactly 6 times.
All inputs are finite; a program needn't handle non-finite values.
Results may differ from the reference program's by a relative error of at most 0.012.
Values may be sent and summed in bfloat16 or wider, within the bound.
A program may use at most 128 MiB of HBM per device.

```python
import math
import jax
import jax.numpy as jnp
import numpy as np
from jax import lax

D = 3584
TOK_DEV = 8
SECTIONS = 2
GROUPS = 4
FF = 256
EXPERTS = 2
TOP = 1
CAP = 6
TOKENS = 128
N_EXPERT = 4


def steps_of(stream_key, extent, split, smallest, top_value):
    factor_of, own = 1.0, jax.random.fold_in(stream_key, 6)
    for axis_at, parts in split:
        steps = jnp.exp(jax.random.uniform(jax.random.fold_in(own, axis_at), (parts,), jnp.float32, smallest / len(split), top_value / len(split)))
        factor_of = factor_of * jnp.repeat(steps, extent[axis_at] // parts).reshape([-1 if axis == axis_at else 1 for axis in range(len(extent))])
    return factor_of


def routed_block(rng, own, number, rows, amount, top, most, lean):
    order = jax.random.permutation(rng, amount)
    crowded, common = load_shares(amount, rows * top, most, lean, True), load_shares(amount, rows * top, most, lean, False)
    places = jnp.arange(amount)

    def named(sizes, turn):
        used = int((sizes > 0).sum())
        fixed = max(1, used // 4)
        moved = fixed + (places - fixed + turn * (used - fixed)) % max(1, amount - fixed)
        return jnp.zeros((amount,), jnp.int32).at[order[jnp.where(places < fixed, places, moved)]].set(jnp.asarray(sizes, jnp.int32))

    sizes = jnp.where(number % 4 == 0, named(crowded, number // 4), named(common, number - number // 4 - 1))
    mixed = jax.random.permutation(jax.random.fold_in(own, 3), amount)
    donor, taker = mixed[0:amount // 2 * 2:2], mixed[1:amount // 2 * 2:2]
    slack = jnp.minimum(sizes[donor] - 1, most - sizes[taker]) // 2
    slack = jnp.where((donor == order[0]) | (taker == order[0]) | (sizes[taker] == 0), 0, jnp.maximum(slack, 0))
    moved = jax.random.randint(jax.random.fold_in(own, 4), (amount // 2,), 0, 1 << 20) % (slack + 1)
    sizes = sizes.at[donor].add(-moved).at[taker].add(moved)
    labels = jnp.searchsorted(jnp.cumsum(sizes), jnp.arange(rows * top), side="right").astype(jnp.int32)
    table = labels.reshape(top, rows).T
    table = table[jax.random.permutation(jax.random.fold_in(own, 1), rows)]
    turn = jax.random.randint(jax.random.fold_in(own, 2), (rows, 1), 0, top)
    return jnp.take_along_axis(table, (jnp.arange(top)[None, :] + turn) % top, axis=1)


def load_shares(amount, total, reach, lean, full):
    loads = [(1 << 20) // math.isqrt(standing ** lean) + 1 for standing in range(1, amount + 1)]
    largest = reach if full else min(reach, max(-(-total // amount), total * loads[0] // sum(loads)))
    least = 1 if total - largest >= amount - 1 else 0
    holding, rest = [largest] + [least] * (amount - 1), total - largest - least * (amount - 1)
    while rest > 0:
        movable = [i for i in range(1, amount) if holding[i] < largest] or [i for i in range(1, amount) if holding[i] < reach]
        whole, left = sum([loads[i] for i in movable]), rest
        for i in movable:
            more = min(reach - holding[i], max(1, left * loads[i] // whole), rest)
            holding[i] = holding[i] + more
            rest = rest - more
    return np.array(holding)


def normal_values(rng, shape, spread, limit, split=(), kind=jnp.bfloat16):
    level = steps_of(rng, shape, split, -0.22, 0.18) if split else 1.0
    array = jax.random.normal(rng, shape, jnp.float32) * spread * level
    return jnp.minimum(jnp.maximum(array, -limit), limit).astype(kind)


def setup_inputs(seed: int = 0) -> dict:
    streams_of = jax.random.split(jax.random.key(seed), 8)
    tokens = normal_values(streams_of[0], (SECTIONS, TOKENS, D), 1.0, 6.0, ((0, 2), (1, 16)))
    grad_out = normal_values(streams_of[1], (SECTIONS, TOKENS, D), 0.25, 1.5, ((0, 2), (1, 16)))
    routes_keys = jax.random.split(jax.random.fold_in(streams_of[2], 1), SECTIONS * TOKENS // TOK_DEV)
    routes_turns = jax.random.permutation(jax.random.fold_in(streams_of[2], 3), SECTIONS * TOKENS // TOK_DEV)
    routes = jax.vmap(lambda own, number: routed_block(jax.random.fold_in(streams_of[2], 2), own, number, TOK_DEV, EXPERTS, TOP, CAP, 2))(routes_keys, routes_turns).reshape((SECTIONS, TOKENS, TOP))
    combine = jnp.clip(jnp.exp(math.log(2.5) - 2.3025851 * jax.random.uniform(streams_of[3], (SECTIONS, TOKENS, TOP), jnp.float32) ** steps_of(streams_of[3], (SECTIONS, TOKENS, TOP), ((0, 2), (1, 16)), -0.2, 0.2)), 0.25, 2.5).astype(jnp.bfloat16)
    w_gate = normal_values(streams_of[4], (SECTIONS, D, EXPERTS * FF), D ** -0.5, 0.09375, ((0, 2), (1, 4), (2, 4)))
    w_up = normal_values(streams_of[5], (SECTIONS, D, EXPERTS * FF), D ** -0.5, 0.09375, ((0, 2), (1, 4), (2, 4)))
    w_down = normal_values(streams_of[6], (SECTIONS, D, EXPERTS * FF), FF ** -0.5, 0.375, ((0, 2), (1, 4), (2, 4)))
    return {"tokens": tokens, "grad_out": grad_out, "routes": routes, "combine": combine, "w_gate": w_gate, "w_up": w_up, "w_down": w_down}


contract_last = (((1,), (1,)), ((), ()))
contract_first = (((0,), (0,)), ((), ()))


def expert_pass(row_inputs, row_cotangent, row_weight, gate_mat, up_mat, down_mat):
    gate_pre = jnp.dot(row_inputs, gate_mat, preferred_element_type=jnp.float32)
    up_pre = jnp.dot(row_inputs, up_mat, preferred_element_type=jnp.float32)
    sigmoid_gate = jax.nn.sigmoid(gate_pre)
    activated = gate_pre * sigmoid_gate
    hidden = (activated * up_pre).astype(jnp.bfloat16)
    expert_out = lax.dot_general(hidden, down_mat, contract_last, preferred_element_type=jnp.float32)
    route_score = jnp.sum(expert_out * row_cotangent.astype(jnp.float32), axis=1)
    out_grad = (row_weight[:, None] * row_cotangent.astype(jnp.float32)).astype(jnp.bfloat16)
    hidden_grad = jnp.dot(out_grad, down_mat, preferred_element_type=jnp.float32)
    gate_grad = (hidden_grad * up_pre * sigmoid_gate * (1.0 + gate_pre * (1.0 - sigmoid_gate))).astype(jnp.bfloat16)
    up_grad = (hidden_grad * activated).astype(jnp.bfloat16)
    input_grad = lax.dot_general(gate_grad, gate_mat, contract_last, preferred_element_type=jnp.float32)
    input_grad = input_grad + lax.dot_general(up_grad, up_mat, contract_last, preferred_element_type=jnp.float32)
    return route_score, input_grad, gate_grad, up_grad, out_grad, hidden


def group_sums(first_factor, second_factor):
    first_groups = first_factor.reshape(N_EXPERT, GROUPS, TOK_DEV, first_factor.shape[1])
    second_groups = second_factor.reshape(N_EXPERT, GROUPS, TOK_DEV, second_factor.shape[1])
    summed = jnp.zeros((first_factor.shape[1], second_factor.shape[1]), jnp.float32)
    for group_index in range(GROUPS):
        first_rows = first_groups[:, group_index].reshape(N_EXPERT * TOK_DEV, first_factor.shape[1])
        second_rows = second_groups[:, group_index].reshape(N_EXPERT * TOK_DEV, second_factor.shape[1])
        partial_value = lax.dot_general(first_rows, second_rows, contract_first, preferred_element_type=jnp.float32)
        rounded = lax.optimization_barrier(partial_value.astype(jnp.bfloat16))
        summed = summed + rounded.astype(jnp.float32)
    return summed


def one_section(section_tokens, section_cotangent, section_routes, section_combine, gate_all, up_all, down_all):
    weights_float = section_combine.astype(jnp.float32)

    def one_expert(carry, expert_index):
        gate_mat = lax.dynamic_slice_in_dim(gate_all, expert_index * FF, FF, 1)
        up_mat = lax.dynamic_slice_in_dim(up_all, expert_index * FF, FF, 1)
        down_mat = lax.dynamic_slice_in_dim(down_all, expert_index * FF, FF, 1)
        chosen = section_routes == expert_index
        row_weight = jnp.sum(jnp.where(chosen, weights_float, 0.0), axis=1)
        route_score, input_grad, gate_grad, up_grad, out_grad, hidden = expert_pass(
            section_tokens, section_cotangent, row_weight, gate_mat, up_mat, down_mat)
        new_carry = (carry[0] + input_grad, carry[1] + jnp.where(chosen, route_score[:, None], 0.0))
        grad_sums = (group_sums(section_tokens, gate_grad), group_sums(section_tokens, up_grad), group_sums(out_grad, hidden))
        return new_carry, grad_sums

    start_carry = (jnp.zeros((TOKENS, D), jnp.float32), jnp.zeros((TOKENS, TOP), jnp.float32))
    final_carry, stacked = lax.scan(one_expert, start_carry, jnp.arange(EXPERTS, dtype=jnp.int32))

    def arrange(stacked_grads):
        return jnp.transpose(stacked_grads, (1, 0, 2)).reshape(D, EXPERTS * FF)

    return final_carry[0], final_carry[1], arrange(stacked[0]), arrange(stacked[1]), arrange(stacked[2])


def reference(tokens, grad_out, routes, combine, w_gate, w_up, w_down):
    input_grads = []
    route_grads = []
    gate_grads = []
    up_grads = []
    down_grads = []
    for section_index in range(SECTIONS):
        results = one_section(tokens[section_index], grad_out[section_index], routes[section_index], combine[section_index],
                            w_gate[section_index], w_up[section_index], w_down[section_index])
        input_grads.append(results[0])
        route_grads.append(results[1])
        gate_grads.append(results[2])
        up_grads.append(results[3])
        down_grads.append(results[4])
    passed = jnp.stack([input_grads[(section_index + 1) % SECTIONS] for section_index in range(SECTIONS)]).astype(jnp.bfloat16)
    return passed, jnp.stack(route_grads), jnp.stack(gate_grads), jnp.stack(up_grads), jnp.stack(down_grads)
```

```python
import functools

import jax
import jax.numpy as jnp
from jax import lax
from jax.experimental import pallas as pl
from jax.experimental.pallas import tpu as pltpu
from jax.sharding import PartitionSpec as P

MESH = pl.DeviceIdType.MESH
F32, BF16 = jnp.float32, jnp.bfloat16
contract_last = (((1,), (1,)), ((), ()))
contract_first = (((0,), (0,)), ((), ()))


def loop(count, step):
    if count <= 4:
        for i in range(count):
            step(i)
    else:
        pl.loop(0, count)(step)


def kernel(
    sizes, tok_ref, go_ref, routes_ref, comb_ref, wg_hbm, wu_hbm, wd_hbm,
    passed_ref, gc_ref, gg_ref, gu_ref, gd_ref,
    stage, xg, wcat, qbuf, hbuf, igsend, igrecv, ssend, srecv, fsend, frecv,
    wsem, p1s, gr, zs, qs, qr, igs, igr, ss, sr, fs, fr,
):
    pipes, E, DP, slices = sizes
    T = tok_ref.shape[1]
    top = routes_ref.shape[2]
    rows, hd = wg_hbm.shape[1:]
    pipe, e, d = (lax.axis_index(a) for a in ("pipe", "expert", "dp"))
    behind = lax.rem(pipe + pipes - 1, pipes)
    ahead = lax.rem(pipe + 1, pipes)
    my_expert = e // slices

    def peer(r):
        return lax.rem(d + r, DP)

    def other(r):
        return lax.rem(e + r, E)

    barrier = pltpu.get_barrier_semaphore()

    def greet(*who):
        pl.semaphore_signal(barrier, inc=1, device_id=who, device_id_type=MESH)

    loop(DP - 1, lambda r: greet(pipe, e, peer(r + 1)))
    loop(E - 1, lambda r: greet(pipe, other(r + 1), d))
    loop(DP, lambda r: greet(ahead, e, r))

    loads = [
        pltpu.make_async_copy(w.at[0], wcat.at[:, pl.ds(i * hd, hd)], wsem.at[i])
        for i, w in enumerate((wg_hbm, wu_hbm, wd_hbm))
    ]
    for c in loads:
        c.start()

    lane = lax.broadcasted_iota(jnp.int32, (T, 128), 1)
    weight = jnp.zeros((T, 128), F32)
    for k in range(top):
        weight = weight + jnp.where(
            routes_ref[0, :, k : k + 1] == lane, comb_ref[0, :, k : k + 1].astype(F32), 0.0
        )
    tail = jnp.concatenate([weight, jnp.zeros_like(weight)], axis=0).astype(BF16)
    for p in range(DP):
        both = jnp.concatenate(
            [
                tok_ref[0, :, p * rows : (p + 1) * rows].astype(F32),
                go_ref[0, :, p * rows : (p + 1) * rows].astype(F32),
            ],
            axis=0,
        ).astype(BF16)
        stage[p, :, :rows] = both
        stage[p, :, rows:] = tail

    pl.semaphore_wait(barrier, 2 * DP - 1 + E - 1)

    def remote(src, dst, send, recv, who):
        return pltpu.make_async_remote_copy(
            src_ref=src, dst_ref=dst, send_sem=send, recv_sem=recv,
            device_id=who, device_id_type=MESH,
        )

    def scatter(r):
        to = peer(r)
        return remote(stage.at[to], xg.at[e * DP + d], p1s.at[r], gr.at[e, d], (pipe, e, to))

    def relay(src, p, way):
        block = xg.at[src * DP + p]
        to = jnp.clip(e + (1 if way == 0 else -1), 0, E - 1)
        return remote(block, block, zs.at[way, src, p], gr.at[src, p], (pipe, to, d))

    def going(src, way):
        if way == 0:
            return jnp.logical_and(src <= e, e + 1 < E)
        return jnp.logical_and(src >= e, e > 0)

    def partial_to(src, r):
        block = qbuf.at[src * DP + d]
        return remote(block, block, qs.at[src, r], qr.at[src, d], (pipe, e, peer(r)))

    def partial_from(src, r):
        p = peer(r)
        block = qbuf.at[src * DP + p]
        return remote(block, block, qs.at[src, r], qr.at[src, p], (pipe, e, p))

    def rows_back(src):
        return remote(igsend.at[src], igrecv.at[e], igs.at[src], igr.at[e], (pipe, src, d))

    def score_back(src):
        return remote(ssend.at[src, d], srecv.at[e], ss.at[src], sr.at[e], (pipe, src, d))

    def rows_in(src):
        return remote(igsend.at[src], igrecv.at[src], igs.at[src], igr.at[src], (pipe, src, d))

    def score_in(src):
        return remote(ssend.at[src, d], srecv.at[src], ss.at[src], sr.at[src], (pipe, src, d))

    def hand_on(p):
        return remote(fsend.at[p], frecv.at[d], fs.at[p], fr.at[d], (behind, e, p))

    def handed(p):
        return remote(fsend.at[p], frecv.at[p], fs.at[p], fr.at[p], (behind, e, p))

    for r in range(1, DP):
        scatter(r).start()
    xg[e * DP + d] = stage[d]

    near = jnp.minimum(e, E - 1 - e)

    def source(i):
        half = (i + 1) // 2
        sign = jnp.where(i % 2 == 1, 1, -1)
        both_sides = e + sign * half
        one_side = jnp.where(e < E - 1 - e, e + (i - near), e - (i - near))
        return jnp.where(i <= 2 * near, both_sides, one_side)

    def arrive(i, first):
        src = e if first else source(i)
        for r in range(DP):
            p = peer(r)
            if not (first and r == 0):
                relay(src, p, 0).wait_recv()
            for way in range(2):
                @pl.when(going(src, way))
                def _():
                    relay(src, p, way).start()
        return src

    def project(src):
        block = xg[pl.ds(src * DP, DP)][:, :, :rows].reshape(DP * 2 * T, rows)
        part = jnp.dot(block, wcat[...], preferred_element_type=F32)
        part = part.reshape(DP, 2 * T, 3 * hd)
        q = jnp.concatenate([part[:, :T, : 2 * hd], part[:, T:, 2 * hd :]], axis=2)
        qbuf[src * DP + d] = q.reshape(DP * T, 3 * hd).astype(BF16)
        for r in range(1, DP):
            partial_to(src, r).start()

    def finish(src, own):
        for r in range(1, DP):
            partial_from(src, r).wait_recv()
        s = qbuf[src * DP].astype(F32)
        for p in range(1, DP):
            s = s + qbuf[src * DP + p].astype(F32)
        w = xg[pl.ds(src * DP, DP)][:, :, rows:].astype(F32)[:, :T].reshape(DP * T, 128)
        at = lax.broadcasted_iota(jnp.int32, (DP * T, 128), 1)
        g = jnp.sum(jnp.where(at == my_expert, w, 0.0), axis=1, keepdims=True)
        gate, up, hg = s[:, :hd], s[:, hd : 2 * hd], s[:, 2 * hd :]
        sig = jax.nn.sigmoid(gate)
        act = gate * sig
        hidden = jnp.where(g > 0.0, (act * up).astype(BF16).astype(F32), 0.0)
        hidden_grad = g * hg
        gate_grad = hidden_grad * up * sig * (1.0 + gate * (1.0 - sig))
        up_grad = hidden_grad * act
        score = jnp.sum(hidden * hg, axis=1, keepdims=True)
        ssend[src] = jnp.broadcast_to(score, (DP * T, 128)).reshape(DP, T, 128)
        both = jnp.concatenate([gate_grad, up_grad], axis=1)
        upper = jnp.concatenate([both, jnp.zeros_like(gate)], axis=1).reshape(DP, T, 3 * hd)
        lower = jnp.concatenate([jnp.zeros_like(both), g * hidden], axis=1).reshape(DP, T, 3 * hd)
        hbuf[pl.ds(src * DP, DP)] = jnp.concatenate([upper, lower], axis=1).astype(BF16)
        ig = lax.dot_general(
            both.astype(BF16), wcat[:, : 2 * hd], contract_last, preferred_element_type=F32
        ).astype(BF16)
        if own:
            igrecv[src] = ig
            srecv[src] = ssend[src, d]
        else:
            igsend[src] = ig
            rows_back(src).start()
            score_back(src).start()

    src = arrive(0, True)
    for c in loads:
        c.wait()
    project(src)
    last = src
    if E <= 4:
        for i in range(1, E):
            src = arrive(i, False)
            project(src)
            finish(last, i == 1)
            last = src
        finish(last, False)
    else:
        finish(src, True)

        @pl.loop(1, E)
        def _(i):
            src = arrive(i, False)
            project(src)
            finish(src, False)

    if E <= 4:
        a = xg[...][:, :, :rows].reshape(E * DP * 2 * T, rows)
        b = hbuf[...].reshape(E * DP * 2 * T, 3 * hd)
        grads = lax.dot_general(a, b, contract_first, preferred_element_type=F32)
        for i, ref in enumerate((gg_ref, gu_ref, gd_ref)):
            ref[0] = grads[:, i * hd : (i + 1) * hd]
    else:
        for ref in (gg_ref, gu_ref, gd_ref):
            ref[0] = jnp.zeros((rows, hd), F32)

        @pl.loop(0, E)
        def _(j):
            a = xg[pl.ds(j * DP, DP)][:, :, :rows].reshape(DP * 2 * T, rows)
            b = hbuf[pl.ds(j * DP, DP)].reshape(DP * 2 * T, 3 * hd)
            grads = lax.dot_general(a, b, contract_first, preferred_element_type=F32)
            for i, ref in enumerate((gg_ref, gu_ref, gd_ref)):
                ref[0] = ref[0] + grads[:, i * hd : (i + 1) * hd]

    def await_back(r):
        rows_in(other(r + 1)).wait_recv()
        score_in(other(r + 1)).wait_recv()

    loop(E - 1, await_back)
    if E <= 4:
        total = igrecv[0].astype(F32)
        for j in range(1, E):
            total = total + igrecv[j].astype(F32)
    else:
        total = lax.fori_loop(
            0, E, lambda j, t: t + igrecv[j].astype(F32), jnp.zeros((DP * T, rows), F32)
        )
    fsend[...] = total.reshape(DP, T, rows).astype(BF16)
    for p in range(DP):
        hand_on(p).start()

    for k in range(top):
        out = jnp.zeros((T, 128), F32)
        for j in range(E):
            if j % slices == 0:
                per = srecv[j]
                for m in range(1, slices):
                    per = per + srecv[j + m]
                out = out + jnp.where(routes_ref[0, :, k : k + 1] == j // slices, per, 0.0)
        gc_ref[0, :, k : k + 1] = out[:, :1]

    for r in range(1, DP):
        scatter(r).wait_send()

    def sent(i):
        src = source(i)
        for r in range(DP):
            for way in range(2):
                @pl.when(going(src, way))
                def _():
                    relay(src, peer(r), way).wait_send()
        for r in range(1, DP):
            partial_to(src, r).wait_send()

    loop(E, sent)

    def sent_back(r):
        rows_back(other(r + 1)).wait_send()
        score_back(other(r + 1)).wait_send()

    loop(E - 1, sent_back)
    for p in range(DP):
        handed(p).wait_recv()
        passed_ref[0, :, p * rows : (p + 1) * rows] = frecv[p]
    for p in range(DP):
        hand_on(p).wait_send()


def solution(mesh):
    pipes, E, DP = (mesh.shape[a] for a in ("pipe", "expert", "dp"))
    slices = min(8, E // 2)

    def body(tokens, grad_out, routes, combine, w_gate, w_up, w_down):
        T, D = tokens.shape[1:]
        top = routes.shape[2]
        rows, hd = w_gate.shape[1:]
        vmem = pl.BlockSpec(memory_space=pltpu.VMEM)
        hbm = pl.BlockSpec(memory_space=pl.ANY)
        dma = pltpu.SemaphoreType.DMA
        grad = jax.ShapeDtypeStruct((1, rows, hd), F32)
        return pl.pallas_call(
            functools.partial(kernel, (pipes, E, DP, slices)),
            out_shape=(
                jax.ShapeDtypeStruct((1, T, D), BF16),
                jax.ShapeDtypeStruct((1, T, top), F32),
                grad, grad, grad,
            ),
            in_specs=[vmem] * 4 + [hbm] * 3,
            out_specs=[vmem] * 5,
            scratch_shapes=[
                pltpu.VMEM((DP, 2 * T, rows + 128), BF16),
                pltpu.VMEM((E * DP, 2 * T, rows + 128), BF16),
                pltpu.VMEM((rows, 3 * hd), BF16),
                pltpu.VMEM((E * DP, DP * T, 3 * hd), BF16),
                pltpu.VMEM((E * DP, 2 * T, 3 * hd), BF16),
                pltpu.VMEM((E, DP * T, rows), BF16),
                pltpu.VMEM((E, DP * T, rows), BF16),
                pltpu.VMEM((E, DP, T, 128), F32),
                pltpu.VMEM((E, T, 128), F32),
                pltpu.VMEM((DP, T, rows), BF16),
                pltpu.VMEM((DP, T, rows), BF16),
                dma((3,)), dma((DP,)), dma((E, DP)), dma((2, E, DP)),
                dma((E, DP)), dma((E, DP)), dma((E,)), dma((E,)),
                dma((E,)), dma((E,)), dma((DP,)), dma((DP,)),
            ],
            compiler_params=pltpu.CompilerParams(
                collective_id=0, has_side_effects=True, vmem_limit_bytes=48 * 2**20
            ),
        )(tokens, grad_out, routes, combine, w_gate, w_up, w_down)

    weights = P("pipe", "dp", "expert")
    mine = P("pipe", ("expert", "dp"), None)
    return jax.shard_map(
        body, mesh=mesh, in_specs=(mine,) * 4 + (weights,) * 3,
        out_specs=(mine, mine, weights, weights, weights), check_vma=False,
    )
```

```python
import functools

import jax
import jax.numpy as jnp
from jax import lax
from jax.experimental import pallas as pl
from jax.experimental.pallas import tpu as pltpu
from jax.sharding import PartitionSpec as P

MESH = pl.DeviceIdType.MESH
F32, BF16 = jnp.float32, jnp.bfloat16
contract_last = (((1,), (1,)), ((), ()))
contract_first = (((0,), (0,)), ((), ()))


def loop(count, step):
    if count <= 4:
        for i in range(count):
            step(i)
    else:
        pl.loop(0, count)(step)


def kernel(
    sizes, tok_hbm, go_hbm, routes_hbm, comb_hbm, wg_hbm, wu_hbm, wd_hbm,
    *rest,
):
    outs, rest = rest[:5], rest[5:]
    passed_ref, gc_ref, gg_ref, gu_ref, gd_ref, osem = rest[:6]
    (
    tok_ref, go_ref, routes_ref, comb_ref, stage, xg, wcat, qbuf, hbuf, igsend, igrecv, ssend, srecv, fsend, frecv,
    isem, wsem, p1s, gr, zs, qs, qr, igs, igr, ss, sr, fs, fr,
    ) = rest[6:]
    pipes, E, DP, slices = sizes
    T = tok_ref.shape[1]
    top = routes_ref.shape[1]
    rows, hd = wg_hbm.shape[1:]
    pipe, e, d = (lax.axis_index(a) for a in ("pipe", "expert", "dp"))
    behind = lax.rem(pipe + pipes - 1, pipes)
    ahead = lax.rem(pipe + 1, pipes)
    my_expert = e // slices

    def peer(r):
        return lax.rem(d + r, DP)

    def other(r):
        return lax.rem(e + r, E)

    barrier = pltpu.get_barrier_semaphore()

    def greet(*who):
        pl.semaphore_signal(barrier, inc=1, device_id=who, device_id_type=MESH)

    loop(DP - 1, lambda r: greet(pipe, e, peer(r + 1)))
    loop(E - 1, lambda r: greet(pipe, other(r + 1), d))
    loop(DP, lambda r: greet(ahead, e, r))

    given = [
        pltpu.make_async_copy(a, b, isem.at[i])
        for i, (a, b) in enumerate(
            (
                (routes_hbm, routes_ref), (comb_hbm, comb_ref),
                (tok_hbm, tok_ref), (go_hbm, go_ref),
            )
        )
    ]
    for c in given:
        c.start()
    loads = [
        pltpu.make_async_copy(w.at[0], wcat.at[:, pl.ds(i * hd, hd)], wsem.at[i])
        for i, w in enumerate((wg_hbm, wu_hbm, wd_hbm))
    ]
    for c in loads:
        c.start()

    lane = lax.broadcasted_iota(jnp.int32, (T, 128), 1)
    diagonal = lane == lax.broadcasted_iota(jnp.int32, (T, 128), 0)
    for c in given[:2]:
        c.wait()

    def column(row):
        spread = jnp.broadcast_to(row, (T, T))
        return jnp.sum(jnp.where(diagonal[:, :T], spread, 0), axis=1, keepdims=True)

    named = [column(routes_ref[0, k : k + 1, :]) for k in range(top)]
    weight = jnp.zeros((T, 128), F32)
    for k in range(top):
        share = column(comb_ref[0, k : k + 1, :].astype(F32))
        weight = weight + jnp.where(named[k] == lane, share, 0.0)
    for c in given[2:]:
        c.wait()
    tail = jnp.concatenate([weight, jnp.zeros_like(weight)], axis=0).astype(BF16)
    for p in range(DP):
        both = jnp.concatenate(
            [
                tok_ref[0, :, p * rows : (p + 1) * rows].astype(F32),
                go_ref[0, :, p * rows : (p + 1) * rows].astype(F32),
            ],
            axis=0,
        ).astype(BF16)
        stage[p, :, :rows] = both
        stage[p, :, rows:] = tail

    pl.semaphore_wait(barrier, 2 * DP - 1 + E - 1)

    def remote(src, dst, send, recv, who):
        return pltpu.make_async_remote_copy(
            src_ref=src, dst_ref=dst, send_sem=send, recv_sem=recv,
            device_id=who, device_id_type=MESH,
        )

    def scatter(r):
        to = peer(r)
        return remote(stage.at[to], xg.at[e * DP + d], p1s.at[r], gr.at[e, d], (pipe, e, to))

    def relay(src, p, way):
        block = xg.at[src * DP + p]
        to = jnp.clip(e + (1 if way == 0 else -1), 0, E - 1)
        return remote(block, block, zs.at[way, src, p], gr.at[src, p], (pipe, to, d))

    def going(src, way):
        if way == 0:
            return jnp.logical_and(src <= e, e + 1 < E)
        return jnp.logical_and(src >= e, e > 0)

    def partial_to(src, r):
        block = qbuf.at[src * DP + d]
        return remote(block, block, qs.at[src, r], qr.at[src, d], (pipe, e, peer(r)))

    def partial_from(src, r):
        p = peer(r)
        block = qbuf.at[src * DP + p]
        return remote(block, block, qs.at[src, r], qr.at[src, p], (pipe, e, p))

    def rows_back(src):
        return remote(igsend.at[src], igrecv.at[e], igs.at[src], igr.at[e], (pipe, src, d))

    def score_back(src):
        return remote(ssend.at[src, d], srecv.at[e], ss.at[src], sr.at[e], (pipe, src, d))

    def rows_in(src):
        return remote(igsend.at[src], igrecv.at[src], igs.at[src], igr.at[src], (pipe, src, d))

    def score_in(src):
        return remote(ssend.at[src, d], srecv.at[src], ss.at[src], sr.at[src], (pipe, src, d))

    def hand_on(p):
        return remote(fsend.at[p], frecv.at[d], fs.at[p], fr.at[d], (behind, e, p))

    def handed(p):
        return remote(fsend.at[p], frecv.at[p], fs.at[p], fr.at[p], (behind, e, p))

    for r in range(1, DP):
        scatter(r).start()
    xg[e * DP + d] = stage[d]

    near = jnp.minimum(e, E - 1 - e)

    def source(i):
        half = (i + 1) // 2
        sign = jnp.where(i % 2 == 1, 1, -1)
        both_sides = e + sign * half
        one_side = jnp.where(e < E - 1 - e, e + (i - near), e - (i - near))
        return jnp.where(i <= 2 * near, both_sides, one_side)

    def arrive(i, first):
        src = e if first else source(i)
        for r in range(DP):
            p = peer(r)
            if not (first and r == 0):
                relay(src, p, 0).wait_recv()
            for way in range(2):
                @pl.when(going(src, way))
                def _():
                    relay(src, p, way).start()
        return src

    def project(src):
        block = xg[pl.ds(src * DP, DP)][:, :, :rows].reshape(DP * 2 * T, rows)
        part = jnp.dot(block, wcat[...], preferred_element_type=F32)
        part = part.reshape(DP, 2 * T, 3 * hd)
        q = jnp.concatenate([part[:, :T, : 2 * hd], part[:, T:, 2 * hd :]], axis=2)
        qbuf[src * DP + d] = q.reshape(DP * T, 3 * hd).astype(BF16)
        for r in range(1, DP):
            partial_to(src, r).start()

    def finish(src, own):
        for r in range(1, DP):
            partial_from(src, r).wait_recv()
        s = qbuf[src * DP].astype(F32)
        for p in range(1, DP):
            s = s + qbuf[src * DP + p].astype(F32)
        w = xg[pl.ds(src * DP, DP)][:, :, rows:].astype(F32)[:, :T].reshape(DP * T, 128)
        at = lax.broadcasted_iota(jnp.int32, (DP * T, 128), 1)
        g = jnp.sum(jnp.where(at == my_expert, w, 0.0), axis=1, keepdims=True)
        gate, up, hg = s[:, :hd], s[:, hd : 2 * hd], s[:, 2 * hd :]
        sig = jax.nn.sigmoid(gate)
        act = gate * sig
        hidden = jnp.where(g > 0.0, (act * up).astype(BF16).astype(F32), 0.0)
        hidden_grad = g * hg
        gate_grad = hidden_grad * up * sig * (1.0 + gate * (1.0 - sig))
        up_grad = hidden_grad * act
        score = jnp.sum(hidden * hg, axis=1, keepdims=True)
        ssend[src] = jnp.broadcast_to(score, (DP * T, 128)).reshape(DP, T, 128)
        both = jnp.concatenate([gate_grad, up_grad], axis=1)
        upper = jnp.concatenate([both, jnp.zeros_like(gate)], axis=1).reshape(DP, T, 3 * hd)
        lower = jnp.concatenate([jnp.zeros_like(both), g * hidden], axis=1).reshape(DP, T, 3 * hd)
        hbuf[pl.ds(src * DP, DP)] = jnp.concatenate([upper, lower], axis=1).astype(BF16)
        ig = lax.dot_general(
            both.astype(BF16), wcat[:, : 2 * hd], contract_last, preferred_element_type=F32
        ).astype(BF16)
        if own:
            igrecv[src] = ig
            srecv[src] = ssend[src, d]
        else:
            igsend[src] = ig
            rows_back(src).start()
            score_back(src).start()

    src = arrive(0, True)
    for c in loads:
        c.wait()
    project(src)
    last = src
    if E <= 4:
        for i in range(1, E):
            src = arrive(i, False)
            project(src)
            finish(last, i == 1)
            last = src
        finish(last, False)
    else:
        finish(src, True)

        @pl.loop(1, E)
        def _(i):
            src = arrive(i, False)
            project(src)
            finish(src, False)

    if E <= 4:
        a = xg[...][:, :, :rows].reshape(E * DP * 2 * T, rows)
        b = hbuf[...].reshape(E * DP * 2 * T, 3 * hd)
        grads = lax.dot_general(a, b, contract_first, preferred_element_type=F32)
        for i, ref in enumerate((gg_ref, gu_ref, gd_ref)):
            ref[0] = grads[:, i * hd : (i + 1) * hd]
    else:
        for ref in (gg_ref, gu_ref, gd_ref):
            ref[0] = jnp.zeros((rows, hd), F32)

        @pl.loop(0, E)
        def _(j):
            a = xg[pl.ds(j * DP, DP)][:, :, :rows].reshape(DP * 2 * T, rows)
            b = hbuf[pl.ds(j * DP, DP)].reshape(DP * 2 * T, 3 * hd)
            grads = lax.dot_general(a, b, contract_first, preferred_element_type=F32)
            for i, ref in enumerate((gg_ref, gu_ref, gd_ref)):
                ref[0] = ref[0] + grads[:, i * hd : (i + 1) * hd]

    results = [
        pltpu.make_async_copy(a, b, osem.at[i])
        for i, (a, b) in enumerate(zip((passed_ref, gc_ref, gg_ref, gu_ref, gd_ref), outs))
    ]
    for c in results[2:]:
        c.start()

    def await_back(r):
        rows_in(other(r + 1)).wait_recv()
        score_in(other(r + 1)).wait_recv()

    loop(E - 1, await_back)
    if E <= 4:
        total = igrecv[0].astype(F32)
        for j in range(1, E):
            total = total + igrecv[j].astype(F32)
    else:
        total = lax.fori_loop(
            0, E, lambda j, t: t + igrecv[j].astype(F32), jnp.zeros((DP * T, rows), F32)
        )
    fsend[...] = total.reshape(DP, T, rows).astype(BF16)
    for p in range(DP):
        hand_on(p).start()

    for k in range(top):
        out = jnp.zeros((T, 128), F32)
        for j in range(E):
            if j % slices == 0:
                per = srecv[j]
                for m in range(1, slices):
                    per = per + srecv[j + m]
                out = out + jnp.where(named[k] == j // slices, per, 0.0)
        row = jnp.sum(jnp.where(diagonal, out, 0.0), axis=0, keepdims=True)
        gc_ref[0, k : k + 1, :] = row[:, :T]
    results[1].start()

    for r in range(1, DP):
        scatter(r).wait_send()

    def sent(i):
        src = source(i)
        for r in range(DP):
            for way in range(2):
                @pl.when(going(src, way))
                def _():
                    relay(src, peer(r), way).wait_send()
        for r in range(1, DP):
            partial_to(src, r).wait_send()

    loop(E, sent)

    def sent_back(r):
        rows_back(other(r + 1)).wait_send()
        score_back(other(r + 1)).wait_send()

    loop(E - 1, sent_back)
    for p in range(DP):
        handed(p).wait_recv()
        passed_ref[0, :, p * rows : (p + 1) * rows] = frecv[p]
    results[0].start()
    for p in range(DP):
        hand_on(p).wait_send()
    for c in results:
        c.wait()


def write_out(*refs):
    count = len(refs) // 2
    sems = refs[-1]
    copies = [
        pltpu.make_async_copy(refs[i], refs[count + i], sems.at[i]) for i in range(count)
    ]
    for c in copies:
        c.start()
    for c in copies:
        c.wait()


def solution(mesh):
    pipes, E, DP = (mesh.shape[a] for a in ("pipe", "expert", "dp"))
    slices = min(8, E // 2)

    def body(tokens, grad_out, routes, combine, w_gate, w_up, w_down):
        T, D = tokens.shape[1:]
        top = routes.shape[2]
        rows, hd = w_gate.shape[1:]
        hbm = pl.BlockSpec(memory_space=pltpu.HBM)
        dma = pltpu.SemaphoreType.DMA
        grad = jax.ShapeDtypeStruct((1, rows, hd), F32)
        shapes = (
            jax.ShapeDtypeStruct((1, T, D), BF16),
            jax.ShapeDtypeStruct((1, top, T), F32),
            grad, grad, grad,
        )
        results = pl.pallas_call(
            functools.partial(kernel, (pipes, E, DP, slices)),
            out_shape=shapes,
            in_specs=[hbm] * 7,
            out_specs=[hbm] * 5,
            scratch_shapes=[
                *(pltpu.VMEM(a.shape, a.dtype) for a in shapes), dma((5,)),
                pltpu.VMEM((1, T, D), BF16),
                pltpu.VMEM((1, T, D), BF16),
                pltpu.VMEM((1, top, T), jnp.int32),
                pltpu.VMEM((1, top, T), BF16),
                pltpu.VMEM((DP, 2 * T, rows + 128), BF16),
                pltpu.VMEM((E * DP, 2 * T, rows + 128), BF16),
                pltpu.VMEM((rows, 3 * hd), BF16),
                pltpu.VMEM((E * DP, DP * T, 3 * hd), BF16),
                pltpu.VMEM((E * DP, 2 * T, 3 * hd), BF16),
                pltpu.VMEM((E, DP * T, rows), BF16),
                pltpu.VMEM((E, DP * T, rows), BF16),
                pltpu.VMEM((E, DP, T, 128), F32),
                pltpu.VMEM((E, T, 128), F32),
                pltpu.VMEM((DP, T, rows), BF16),
                pltpu.VMEM((DP, T, rows), BF16),
                dma((4,)), dma((3,)), dma((DP,)), dma((E, DP)), dma((2, E, DP)),
                dma((E, DP)), dma((E, DP)), dma((E,)), dma((E,)),
                dma((E,)), dma((E,)), dma((DP,)), dma((DP,)),
            ],
            compiler_params=pltpu.CompilerParams(
                collective_id=0, has_side_effects=True, vmem_limit_bytes=64 * 2**20
            ),
        )(
            tokens, grad_out, jnp.swapaxes(routes, 1, 2), jnp.swapaxes(combine, 1, 2),
            w_gate, w_up, w_down,
        )
        passed, grad_combine, *grads = pl.pallas_call(
            write_out,
            out_shape=shapes,
            in_specs=[hbm] * 5,
            out_specs=[hbm] * 5,
            scratch_shapes=[dma((5,))],
            compiler_params=pltpu.CompilerParams(vmem_limit_bytes=64 * 2**20),
        )(*results)
        return (passed, jnp.swapaxes(grad_combine, 1, 2), *grads)

    weights = P("pipe", "dp", "expert")
    mine = P("pipe", ("expert", "dp"), None)
    return jax.shard_map(
        body, mesh=mesh, in_specs=(mine,) * 4 + (weights,) * 3,
        out_specs=(mine, mine, weights, weights, weights), check_vma=False,
    )
```

```python
import functools

import jax
import jax.numpy as jnp
from jax import lax
from jax.experimental import pallas as pl
from jax.experimental.pallas import tpu as pltpu
from jax.sharding import PartitionSpec as P

MESH = pl.DeviceIdType.MESH
F32, BF16 = jnp.float32, jnp.bfloat16
contract_last = (((1,), (1,)), ((), ()))
contract_first = (((0,), (0,)), ((), ()))


def loop(count, step):
    if count <= 4:
        for i in range(count):
            step(i)
    else:
        pl.loop(0, count)(step)


def kernel(
    sizes, tok_hbm, go_hbm, routes_hbm, comb_hbm, wg_hbm, wu_hbm, wd_hbm,
    passed_ref, gc_ref, gg_ref, gu_ref, gd_ref,
    tok_ref, go_ref, routes_ref, comb_ref, stage, xg, wcat, qbuf, hbuf, igsend, igrecv, ssend, srecv, fsend, frecv,
    isem, wsem, p1s, gr, zs, qs, qr, igs, igr, ss, sr, fs, fr,
):
    pipes, E, DP, slices = sizes
    T = tok_ref.shape[1]
    top = routes_ref.shape[1]
    rows, hd = wg_hbm.shape[1:]
    pipe, e, d = (lax.axis_index(a) for a in ("pipe", "expert", "dp"))
    behind = lax.rem(pipe + pipes - 1, pipes)
    ahead = lax.rem(pipe + 1, pipes)
    my_expert = e // slices

    def peer(r):
        return lax.rem(d + r, DP)

    def other(r):
        return lax.rem(e + r, E)

    barrier = pltpu.get_barrier_semaphore()

    def greet(*who):
        pl.semaphore_signal(barrier, inc=1, device_id=who, device_id_type=MESH)

    loop(DP - 1, lambda r: greet(pipe, e, peer(r + 1)))
    loop(E - 1, lambda r: greet(pipe, other(r + 1), d))
    loop(DP, lambda r: greet(ahead, e, r))

    given = [
        pltpu.make_async_copy(a, b, isem.at[i])
        for i, (a, b) in enumerate(
            (
                (routes_hbm, routes_ref), (comb_hbm, comb_ref),
                (tok_hbm, tok_ref), (go_hbm, go_ref),
            )
        )
    ]
    for c in given:
        c.start()
    loads = [
        pltpu.make_async_copy(w.at[0], wcat.at[:, pl.ds(i * hd, hd)], wsem.at[i])
        for i, w in enumerate((wg_hbm, wu_hbm, wd_hbm))
    ]
    for c in loads:
        c.start()

    lane = lax.broadcasted_iota(jnp.int32, (T, 128), 1)
    diagonal = lane == lax.broadcasted_iota(jnp.int32, (T, 128), 0)
    for c in given[:2]:
        c.wait()

    def column(row):
        spread = jnp.broadcast_to(row, (T, T))
        return jnp.sum(jnp.where(diagonal[:, :T], spread, 0), axis=1, keepdims=True)

    named = [column(routes_ref[0, k : k + 1, :]) for k in range(top)]
    weight = jnp.zeros((T, 128), F32)
    for k in range(top):
        share = column(comb_ref[0, k : k + 1, :].astype(F32))
        weight = weight + jnp.where(named[k] == lane, share, 0.0)
    for c in given[2:]:
        c.wait()
    tail = jnp.concatenate([weight, jnp.zeros_like(weight)], axis=0).astype(BF16)
    for p in range(DP):
        both = jnp.concatenate(
            [
                tok_ref[0, :, p * rows : (p + 1) * rows].astype(F32),
                go_ref[0, :, p * rows : (p + 1) * rows].astype(F32),
            ],
            axis=0,
        ).astype(BF16)
        stage[p, :, :rows] = both
        stage[p, :, rows:] = tail

    pl.semaphore_wait(barrier, 2 * DP - 1 + E - 1)

    def remote(src, dst, send, recv, who):
        return pltpu.make_async_remote_copy(
            src_ref=src, dst_ref=dst, send_sem=send, recv_sem=recv,
            device_id=who, device_id_type=MESH,
        )

    def scatter(r):
        to = peer(r)
        return remote(stage.at[to], xg.at[e * DP + d], p1s.at[r], gr.at[e, d], (pipe, e, to))

    def relay(src, p, way):
        block = xg.at[src * DP + p]
        to = jnp.clip(e + (1 if way == 0 else -1), 0, E - 1)
        return remote(block, block, zs.at[way, src, p], gr.at[src, p], (pipe, to, d))

    def going(src, way):
        if way == 0:
            return jnp.logical_and(src <= e, e + 1 < E)
        return jnp.logical_and(src >= e, e > 0)

    def partial_to(src, r):
        block = qbuf.at[src * DP + d]
        return remote(block, block, qs.at[src, r], qr.at[src, d], (pipe, e, peer(r)))

    def partial_from(src, r):
        p = peer(r)
        block = qbuf.at[src * DP + p]
        return remote(block, block, qs.at[src, r], qr.at[src, p], (pipe, e, p))

    def rows_back(src):
        return remote(igsend.at[src], igrecv.at[e], igs.at[src], igr.at[e], (pipe, src, d))

    def score_back(src):
        return remote(ssend.at[src, d], srecv.at[e], ss.at[src], sr.at[e], (pipe, src, d))

    def rows_in(src):
        return remote(igsend.at[src], igrecv.at[src], igs.at[src], igr.at[src], (pipe, src, d))

    def score_in(src):
        return remote(ssend.at[src, d], srecv.at[src], ss.at[src], sr.at[src], (pipe, src, d))

    def hand_on(p):
        return remote(fsend.at[p], frecv.at[d], fs.at[p], fr.at[d], (behind, e, p))

    def handed(p):
        return remote(fsend.at[p], frecv.at[p], fs.at[p], fr.at[p], (behind, e, p))

    for r in range(1, DP):
        scatter(r).start()
    xg[e * DP + d] = stage[d]

    near = jnp.minimum(e, E - 1 - e)

    def source(i):
        half = (i + 1) // 2
        sign = jnp.where(i % 2 == 1, 1, -1)
        both_sides = e + sign * half
        one_side = jnp.where(e < E - 1 - e, e + (i - near), e - (i - near))
        return jnp.where(i <= 2 * near, both_sides, one_side)

    def arrive(i, first):
        src = e if first else source(i)
        for r in range(DP):
            p = peer(r)
            if not (first and r == 0):
                relay(src, p, 0).wait_recv()
            for way in range(2):
                @pl.when(going(src, way))
                def _():
                    relay(src, p, way).start()
        return src

    def project(src):
        block = xg[pl.ds(src * DP, DP)][:, :, :rows].reshape(DP * 2 * T, rows)
        part = jnp.dot(block, wcat[...], preferred_element_type=F32)
        part = part.reshape(DP, 2 * T, 3 * hd)
        q = jnp.concatenate([part[:, :T, : 2 * hd], part[:, T:, 2 * hd :]], axis=2)
        qbuf[src * DP + d] = q.reshape(DP * T, 3 * hd).astype(BF16)
        for r in range(1, DP):
            partial_to(src, r).start()

    def finish(src, own):
        for r in range(1, DP):
            partial_from(src, r).wait_recv()
        s = qbuf[src * DP].astype(F32)
        for p in range(1, DP):
            s = s + qbuf[src * DP + p].astype(F32)
        w = xg[pl.ds(src * DP, DP)][:, :, rows:].astype(F32)[:, :T].reshape(DP * T, 128)
        at = lax.broadcasted_iota(jnp.int32, (DP * T, 128), 1)
        g = jnp.sum(jnp.where(at == my_expert, w, 0.0), axis=1, keepdims=True)
        gate, up, hg = s[:, :hd], s[:, hd : 2 * hd], s[:, 2 * hd :]
        sig = jax.nn.sigmoid(gate)
        act = gate * sig
        hidden = jnp.where(g > 0.0, (act * up).astype(BF16).astype(F32), 0.0)
        hidden_grad = g * hg
        gate_grad = hidden_grad * up * sig * (1.0 + gate * (1.0 - sig))
        up_grad = hidden_grad * act
        score = jnp.sum(hidden * hg, axis=1, keepdims=True)
        ssend[src] = jnp.broadcast_to(score, (DP * T, 128)).reshape(DP, T, 128)
        both = jnp.concatenate([gate_grad, up_grad], axis=1)
        upper = jnp.concatenate([both, jnp.zeros_like(gate)], axis=1).reshape(DP, T, 3 * hd)
        lower = jnp.concatenate([jnp.zeros_like(both), g * hidden], axis=1).reshape(DP, T, 3 * hd)
        hbuf[pl.ds(src * DP, DP)] = jnp.concatenate([upper, lower], axis=1).astype(BF16)
        ig = lax.dot_general(
            both.astype(BF16), wcat[:, : 2 * hd], contract_last, preferred_element_type=F32
        ).astype(BF16)
        if own:
            igrecv[src] = ig
            srecv[src] = ssend[src, d]
        else:
            igsend[src] = ig
            rows_back(src).start()
            score_back(src).start()

    src = arrive(0, True)
    for c in loads:
        c.wait()
    project(src)
    last = src
    if E <= 4:
        for i in range(1, E):
            src = arrive(i, False)
            project(src)
            finish(last, i == 1)
            last = src
        finish(last, False)
    else:
        finish(src, True)

        @pl.loop(1, E)
        def _(i):
            src = arrive(i, False)
            project(src)
            finish(src, False)

    if E <= 4:
        a = xg[...][:, :, :rows].reshape(E * DP * 2 * T, rows)
        b = hbuf[...].reshape(E * DP * 2 * T, 3 * hd)
        grads = lax.dot_general(a, b, contract_first, preferred_element_type=F32)
        for i, ref in enumerate((gg_ref, gu_ref, gd_ref)):
            ref[0] = grads[:, i * hd : (i + 1) * hd]
    else:
        for ref in (gg_ref, gu_ref, gd_ref):
            ref[0] = jnp.zeros((rows, hd), F32)

        @pl.loop(0, E)
        def _(j):
            a = xg[pl.ds(j * DP, DP)][:, :, :rows].reshape(DP * 2 * T, rows)
            b = hbuf[pl.ds(j * DP, DP)].reshape(DP * 2 * T, 3 * hd)
            grads = lax.dot_general(a, b, contract_first, preferred_element_type=F32)
            for i, ref in enumerate((gg_ref, gu_ref, gd_ref)):
                ref[0] = ref[0] + grads[:, i * hd : (i + 1) * hd]

    def await_back(r):
        rows_in(other(r + 1)).wait_recv()
        score_in(other(r + 1)).wait_recv()

    loop(E - 1, await_back)
    if E <= 4:
        total = igrecv[0].astype(F32)
        for j in range(1, E):
            total = total + igrecv[j].astype(F32)
    else:
        total = lax.fori_loop(
            0, E, lambda j, t: t + igrecv[j].astype(F32), jnp.zeros((DP * T, rows), F32)
        )
    fsend[...] = total.reshape(DP, T, rows).astype(BF16)
    for p in range(DP):
        hand_on(p).start()

    for k in range(top):
        out = jnp.zeros((T, 128), F32)
        for j in range(E):
            if j % slices == 0:
                per = srecv[j]
                for m in range(1, slices):
                    per = per + srecv[j + m]
                out = out + jnp.where(named[k] == j // slices, per, 0.0)
        row = jnp.sum(jnp.where(diagonal, out, 0.0), axis=0, keepdims=True)
        gc_ref[0, k : k + 1, :] = row[:, :T]

    for r in range(1, DP):
        scatter(r).wait_send()

    def sent(i):
        src = source(i)
        for r in range(DP):
            for way in range(2):
                @pl.when(going(src, way))
                def _():
                    relay(src, peer(r), way).wait_send()
        for r in range(1, DP):
            partial_to(src, r).wait_send()

    loop(E, sent)

    def sent_back(r):
        rows_back(other(r + 1)).wait_send()
        score_back(other(r + 1)).wait_send()

    loop(E - 1, sent_back)
    for p in range(DP):
        handed(p).wait_recv()
        passed_ref[0, :, p * rows : (p + 1) * rows] = frecv[p]
    for p in range(DP):
        hand_on(p).wait_send()


def write_out(*refs):
    count = len(refs) // 2
    sems = refs[-1]
    copies = [
        pltpu.make_async_copy(refs[i], refs[count + i], sems.at[i]) for i in range(count)
    ]
    for c in copies:
        c.start()
    for c in copies:
        c.wait()


def solution(mesh):
    pipes, E, DP = (mesh.shape[a] for a in ("pipe", "expert", "dp"))
    slices = min(8, E // 2)

    def body(tokens, grad_out, routes, combine, w_gate, w_up, w_down):
        T, D = tokens.shape[1:]
        top = routes.shape[2]
        rows, hd = w_gate.shape[1:]
        vmem = pl.BlockSpec(memory_space=pltpu.VMEM)
        hbm = pl.BlockSpec(memory_space=pltpu.HBM)
        dma = pltpu.SemaphoreType.DMA
        grad = jax.ShapeDtypeStruct((1, rows, hd), F32)
        shapes = (
            jax.ShapeDtypeStruct((1, T, D), BF16),
            jax.ShapeDtypeStruct((1, top, T), F32),
            grad, grad, grad,
        )
        results = pl.pallas_call(
            functools.partial(kernel, (pipes, E, DP, slices)),
            out_shape=shapes,
            in_specs=[hbm] * 7,
            out_specs=[vmem] * 5,
            scratch_shapes=[
                pltpu.VMEM((1, T, D), BF16),
                pltpu.VMEM((1, T, D), BF16),
                pltpu.VMEM((1, top, T), jnp.int32),
                pltpu.VMEM((1, top, T), BF16),
                pltpu.VMEM((DP, 2 * T, rows + 128), BF16),
                pltpu.VMEM((E * DP, 2 * T, rows + 128), BF16),
                pltpu.VMEM((rows, 3 * hd), BF16),
                pltpu.VMEM((E * DP, DP * T, 3 * hd), BF16),
                pltpu.VMEM((E * DP, 2 * T, 3 * hd), BF16),
                pltpu.VMEM((E, DP * T, rows), BF16),
                pltpu.VMEM((E, DP * T, rows), BF16),
                pltpu.VMEM((E, DP, T, 128), F32),
                pltpu.VMEM((E, T, 128), F32),
                pltpu.VMEM((DP, T, rows), BF16),
                pltpu.VMEM((DP, T, rows), BF16),
                dma((4,)), dma((3,)), dma((DP,)), dma((E, DP)), dma((2, E, DP)),
                dma((E, DP)), dma((E, DP)), dma((E,)), dma((E,)),
                dma((E,)), dma((E,)), dma((DP,)), dma((DP,)),
            ],
            compiler_params=pltpu.CompilerParams(
                collective_id=0, has_side_effects=True, vmem_limit_bytes=48 * 2**20
            ),
        )(
            *(
                pltpu.with_memory_space_constraint(a, pltpu.HBM)
                for a in (
                    tokens, grad_out, jnp.swapaxes(routes, 1, 2), jnp.swapaxes(combine, 1, 2),
                    w_gate, w_up, w_down,
                )
            )
        )
        passed, grad_combine, *grads = pl.pallas_call(
            write_out,
            out_shape=shapes,
            in_specs=[vmem] * 5,
            out_specs=[hbm] * 5,
            scratch_shapes=[dma((5,))],
        )(*results)
        return (passed, jnp.swapaxes(grad_combine, 1, 2), *grads)

    weights = P("pipe", "dp", "expert")
    mine = P("pipe", ("expert", "dp"), None)
    return jax.shard_map(
        body, mesh=mesh, in_specs=(mine,) * 4 + (weights,) * 3,
        out_specs=(mine, mine, weights, weights, weights), check_vma=False,
    )
```

```python
import functools

import jax
import jax.numpy as jnp
from jax import lax
from jax.experimental import pallas as pl
from jax.experimental.pallas import tpu as pltpu
from jax.sharding import PartitionSpec as P

MESH = pl.DeviceIdType.MESH
F32, BF16 = jnp.float32, jnp.bfloat16
contract_last = (((1,), (1,)), ((), ()))
contract_first = (((0,), (0,)), ((), ()))


def loop(count, step):
    if count <= 4:
        for i in range(count):
            step(i)
    else:
        pl.loop(0, count)(step)


def kernel(
    sizes, tok_hbm, go_hbm, routes_hbm, comb_hbm, wg_hbm, wu_hbm, wd_hbm,
    passed_ref, gc_ref, gg_ref, gu_ref, gd_ref,
    tok_ref, go_ref, routes_ref, comb_ref, stage, xg, wcat, qbuf, hbuf, igsend, igrecv, ssend, srecv, fsend, frecv,
    isem, wsem, p1s, gr, zs, qs, qr, igs, igr, ss, sr, fs, fr,
):
    pipes, E, DP, slices = sizes
    T = tok_ref.shape[1]
    top = routes_ref.shape[1]
    rows, hd = wg_hbm.shape[1:]
    pipe, e, d = (lax.axis_index(a) for a in ("pipe", "expert", "dp"))
    behind = lax.rem(pipe + pipes - 1, pipes)
    ahead = lax.rem(pipe + 1, pipes)
    my_expert = e // slices

    def peer(r):
        return lax.rem(d + r, DP)

    def other(r):
        return lax.rem(e + r, E)

    barrier = pltpu.get_barrier_semaphore()

    def greet(*who):
        pl.semaphore_signal(barrier, inc=1, device_id=who, device_id_type=MESH)

    loop(DP - 1, lambda r: greet(pipe, e, peer(r + 1)))
    loop(E - 1, lambda r: greet(pipe, other(r + 1), d))
    loop(DP, lambda r: greet(ahead, e, r))

    given = [
        pltpu.make_async_copy(a, b, isem.at[i])
        for i, (a, b) in enumerate(
            (
                (routes_hbm, routes_ref), (comb_hbm, comb_ref),
                (tok_hbm, tok_ref), (go_hbm, go_ref),
            )
        )
    ]
    for c in given:
        c.start()
    loads = [
        pltpu.make_async_copy(w.at[0], wcat.at[:, pl.ds(i * hd, hd)], wsem.at[i])
        for i, w in enumerate((wg_hbm, wu_hbm, wd_hbm))
    ]
    for c in loads:
        c.start()

    lane = lax.broadcasted_iota(jnp.int32, (T, 128), 1)
    diagonal = lane == lax.broadcasted_iota(jnp.int32, (T, 128), 0)
    for c in given[:2]:
        c.wait()

    def column(row):
        spread = jnp.broadcast_to(row, (T, T))
        return jnp.sum(jnp.where(diagonal[:, :T], spread, 0), axis=1, keepdims=True)

    named = [column(routes_ref[0, k : k + 1, :]) for k in range(top)]
    weight = jnp.zeros((T, 128), F32)
    for k in range(top):
        share = column(comb_ref[0, k : k + 1, :].astype(F32))
        weight = weight + jnp.where(named[k] == lane, share, 0.0)
    for c in given[2:]:
        c.wait()
    tail = jnp.concatenate([weight, jnp.zeros_like(weight)], axis=0).astype(BF16)
    for p in range(DP):
        both = jnp.concatenate(
            [
                tok_ref[0, :, p * rows : (p + 1) * rows].astype(F32),
                go_ref[0, :, p * rows : (p + 1) * rows].astype(F32),
            ],
            axis=0,
        ).astype(BF16)
        stage[p, :, :rows] = both
        stage[p, :, rows:] = tail

    pl.semaphore_wait(barrier, 2 * DP - 1 + E - 1)

    def remote(src, dst, send, recv, who):
        return pltpu.make_async_remote_copy(
            src_ref=src, dst_ref=dst, send_sem=send, recv_sem=recv,
            device_id=who, device_id_type=MESH,
        )

    def scatter(r):
        to = peer(r)
        return remote(stage.at[to], xg.at[e * DP + d], p1s.at[r], gr.at[e, d], (pipe, e, to))

    def relay(src, p, way):
        block = xg.at[src * DP + p]
        to = jnp.clip(e + (1 if way == 0 else -1), 0, E - 1)
        return remote(block, block, zs.at[way, src, p], gr.at[src, p], (pipe, to, d))

    def going(src, way):
        if way == 0:
            return jnp.logical_and(src <= e, e + 1 < E)
        return jnp.logical_and(src >= e, e > 0)

    def partial_to(src, r):
        block = qbuf.at[src * DP + d]
        return remote(block, block, qs.at[src, r], qr.at[src, d], (pipe, e, peer(r)))

    def partial_from(src, r):
        p = peer(r)
        block = qbuf.at[src * DP + p]
        return remote(block, block, qs.at[src, r], qr.at[src, p], (pipe, e, p))

    def rows_back(src):
        return remote(igsend.at[src], igrecv.at[e], igs.at[src], igr.at[e], (pipe, src, d))

    def score_back(src):
        return remote(ssend.at[src, d], srecv.at[e], ss.at[src], sr.at[e], (pipe, src, d))

    def rows_in(src):
        return remote(igsend.at[src], igrecv.at[src], igs.at[src], igr.at[src], (pipe, src, d))

    def score_in(src):
        return remote(ssend.at[src, d], srecv.at[src], ss.at[src], sr.at[src], (pipe, src, d))

    def hand_on(p):
        return remote(fsend.at[p], frecv.at[d], fs.at[p], fr.at[d], (behind, e, p))

    def handed(p):
        return remote(fsend.at[p], frecv.at[p], fs.at[p], fr.at[p], (behind, e, p))

    for r in range(1, DP):
        scatter(r).start()
    xg[e * DP + d] = stage[d]

    near = jnp.minimum(e, E - 1 - e)

    def source(i):
        half = (i + 1) // 2
        sign = jnp.where(i % 2 == 1, 1, -1)
        both_sides = e + sign * half
        one_side = jnp.where(e < E - 1 - e, e + (i - near), e - (i - near))
        return jnp.where(i <= 2 * near, both_sides, one_side)

    def arrive(i, first):
        src = e if first else source(i)
        for r in range(DP):
            p = peer(r)
            if not (first and r == 0):
                relay(src, p, 0).wait_recv()
            for way in range(2):
                @pl.when(going(src, way))
                def _():
                    relay(src, p, way).start()
        return src

    def project(src):
        block = xg[pl.ds(src * DP, DP)][:, :, :rows].reshape(DP * 2 * T, rows)
        part = jnp.dot(block, wcat[...], preferred_element_type=F32)
        part = part.reshape(DP, 2 * T, 3 * hd)
        q = jnp.concatenate([part[:, :T, : 2 * hd], part[:, T:, 2 * hd :]], axis=2)
        qbuf[src * DP + d] = q.reshape(DP * T, 3 * hd).astype(BF16)
        for r in range(1, DP):
            partial_to(src, r).start()

    def finish(src, own):
        for r in range(1, DP):
            partial_from(src, r).wait_recv()
        s = qbuf[src * DP].astype(F32)
        for p in range(1, DP):
            s = s + qbuf[src * DP + p].astype(F32)
        w = xg[pl.ds(src * DP, DP)][:, :, rows:].astype(F32)[:, :T].reshape(DP * T, 128)
        at = lax.broadcasted_iota(jnp.int32, (DP * T, 128), 1)
        g = jnp.sum(jnp.where(at == my_expert, w, 0.0), axis=1, keepdims=True)
        gate, up, hg = s[:, :hd], s[:, hd : 2 * hd], s[:, 2 * hd :]
        sig = jax.nn.sigmoid(gate)
        act = gate * sig
        hidden = jnp.where(g > 0.0, (act * up).astype(BF16).astype(F32), 0.0)
        hidden_grad = g * hg
        gate_grad = hidden_grad * up * sig * (1.0 + gate * (1.0 - sig))
        up_grad = hidden_grad * act
        score = jnp.sum(hidden * hg, axis=1, keepdims=True)
        ssend[src] = jnp.broadcast_to(score, (DP * T, 128)).reshape(DP, T, 128)
        both = jnp.concatenate([gate_grad, up_grad], axis=1)
        upper = jnp.concatenate([both, jnp.zeros_like(gate)], axis=1).reshape(DP, T, 3 * hd)
        lower = jnp.concatenate([jnp.zeros_like(both), g * hidden], axis=1).reshape(DP, T, 3 * hd)
        hbuf[pl.ds(src * DP, DP)] = jnp.concatenate([upper, lower], axis=1).astype(BF16)
        ig = lax.dot_general(
            both.astype(BF16), wcat[:, : 2 * hd], contract_last, preferred_element_type=F32
        ).astype(BF16)
        if own:
            igrecv[src] = ig
            srecv[src] = ssend[src, d]
        else:
            igsend[src] = ig
            rows_back(src).start()
            score_back(src).start()

    src = arrive(0, True)
    for c in loads:
        c.wait()
    project(src)
    last = src
    if E <= 4:
        for i in range(1, E):
            src = arrive(i, False)
            project(src)
            finish(last, i == 1)
            last = src
        finish(last, False)
    else:
        finish(src, True)

        @pl.loop(1, E)
        def _(i):
            src = arrive(i, False)
            project(src)
            finish(src, False)

    if E <= 4:
        a = xg[...][:, :, :rows].reshape(E * DP * 2 * T, rows)
        b = hbuf[...].reshape(E * DP * 2 * T, 3 * hd)
        grads = lax.dot_general(a, b, contract_first, preferred_element_type=F32)
        for i, ref in enumerate((gg_ref, gu_ref, gd_ref)):
            ref[0] = grads[:, i * hd : (i + 1) * hd]
    else:
        for ref in (gg_ref, gu_ref, gd_ref):
            ref[0] = jnp.zeros((rows, hd), F32)

        @pl.loop(0, E)
        def _(j):
            a = xg[pl.ds(j * DP, DP)][:, :, :rows].reshape(DP * 2 * T, rows)
            b = hbuf[pl.ds(j * DP, DP)].reshape(DP * 2 * T, 3 * hd)
            grads = lax.dot_general(a, b, contract_first, preferred_element_type=F32)
            for i, ref in enumerate((gg_ref, gu_ref, gd_ref)):
                ref[0] = ref[0] + grads[:, i * hd : (i + 1) * hd]

    def await_back(r):
        rows_in(other(r + 1)).wait_recv()
        score_in(other(r + 1)).wait_recv()

    loop(E - 1, await_back)
    if E <= 4:
        total = igrecv[0].astype(F32)
        for j in range(1, E):
            total = total + igrecv[j].astype(F32)
    else:
        total = lax.fori_loop(
            0, E, lambda j, t: t + igrecv[j].astype(F32), jnp.zeros((DP * T, rows), F32)
        )
    fsend[...] = total.reshape(DP, T, rows).astype(BF16)
    for p in range(DP):
        hand_on(p).start()

    for k in range(top):
        out = jnp.zeros((T, 128), F32)
        for j in range(E):
            if j % slices == 0:
                per = srecv[j]
                for m in range(1, slices):
                    per = per + srecv[j + m]
                out = out + jnp.where(named[k] == j // slices, per, 0.0)
        row = jnp.sum(jnp.where(diagonal, out, 0.0), axis=0, keepdims=True)
        gc_ref[0, k : k + 1, :] = row[:, :T]

    for r in range(1, DP):
        scatter(r).wait_send()

    def sent(i):
        src = source(i)
        for r in range(DP):
            for way in range(2):
                @pl.when(going(src, way))
                def _():
                    relay(src, peer(r), way).wait_send()
        for r in range(1, DP):
            partial_to(src, r).wait_send()

    loop(E, sent)

    def sent_back(r):
        rows_back(other(r + 1)).wait_send()
        score_back(other(r + 1)).wait_send()

    loop(E - 1, sent_back)
    for p in range(DP):
        handed(p).wait_recv()
        passed_ref[0, :, p * rows : (p + 1) * rows] = frecv[p]
    for p in range(DP):
        hand_on(p).wait_send()


def write_out(*refs):
    count = len(refs) // 2
    sems = refs[-1]
    copies = [
        pltpu.make_async_copy(refs[i], refs[count + i], sems.at[i]) for i in range(count)
    ]
    for c in copies:
        c.start()
    for c in copies:
        c.wait()


def solution(mesh):
    pipes, E, DP = (mesh.shape[a] for a in ("pipe", "expert", "dp"))
    slices = min(8, E // 2)

    def body(tokens, grad_out, routes, combine, w_gate, w_up, w_down):
        T, D = tokens.shape[1:]
        top = routes.shape[2]
        rows, hd = w_gate.shape[1:]
        vmem = pl.BlockSpec(memory_space=pltpu.VMEM)
        hbm = pl.BlockSpec(memory_space=pltpu.HBM)
        dma = pltpu.SemaphoreType.DMA
        grad = jax.ShapeDtypeStruct((1, rows, hd), F32)
        shapes = (
            jax.ShapeDtypeStruct((1, T, D), BF16),
            jax.ShapeDtypeStruct((1, top, T), F32),
            grad, grad, grad,
        )
        results = pl.pallas_call(
            functools.partial(kernel, (pipes, E, DP, slices)),
            out_shape=shapes,
            in_specs=[hbm] * 7,
            out_specs=[vmem] * 5,
            scratch_shapes=[
                pltpu.VMEM((1, T, D), BF16),
                pltpu.VMEM((1, T, D), BF16),
                pltpu.VMEM((1, top, T), jnp.int32),
                pltpu.VMEM((1, top, T), BF16),
                pltpu.VMEM((DP, 2 * T, rows + 128), BF16),
                pltpu.VMEM((E * DP, 2 * T, rows + 128), BF16),
                pltpu.VMEM((rows, 3 * hd), BF16),
                pltpu.VMEM((E * DP, DP * T, 3 * hd), BF16),
                pltpu.VMEM((E * DP, 2 * T, 3 * hd), BF16),
                pltpu.VMEM((E, DP * T, rows), BF16),
                pltpu.VMEM((E, DP * T, rows), BF16),
                pltpu.VMEM((E, DP, T, 128), F32),
                pltpu.VMEM((E, T, 128), F32),
                pltpu.VMEM((DP, T, rows), BF16),
                pltpu.VMEM((DP, T, rows), BF16),
                dma((4,)), dma((3,)), dma((DP,)), dma((E, DP)), dma((2, E, DP)),
                dma((E, DP)), dma((E, DP)), dma((E,)), dma((E,)),
                dma((E,)), dma((E,)), dma((DP,)), dma((DP,)),
            ],
            compiler_params=pltpu.CompilerParams(
                collective_id=0, has_side_effects=True, vmem_limit_bytes=48 * 2**20
            ),
        )(
            *(
                pltpu.with_memory_space_constraint(a, pltpu.HBM)
                for a in (
                    tokens, grad_out, jnp.swapaxes(routes, 1, 2), jnp.swapaxes(combine, 1, 2),
                    w_gate, w_up, w_down,
                )
            )
        )
        passed, grad_combine, *grads = pl.pallas_call(
            write_out,
            out_shape=shapes,
            in_specs=[vmem] * 5,
            out_specs=[hbm] * 5,
            scratch_shapes=[dma((5,))],
            compiler_params=pltpu.CompilerParams(vmem_limit_bytes=2 * 2**20),
        )(*results)
        return (passed, jnp.swapaxes(grad_combine, 1, 2), *grads)

    weights = P("pipe", "dp", "expert")
    mine = P("pipe", ("expert", "dp"), None)
    return jax.shard_map(
        body, mesh=mesh, in_specs=(mine,) * 4 + (weights,) * 3,
        out_specs=(mine, mine, weights, weights, weights), check_vma=False,
    )
```

```python
import functools

import jax
import jax.numpy as jnp
from jax import lax
from jax.experimental import pallas as pl
from jax.experimental.pallas import tpu as pltpu
from jax.sharding import PartitionSpec as P

MESH = pl.DeviceIdType.MESH
F32, BF16 = jnp.float32, jnp.bfloat16
contract_last = (((1,), (1,)), ((), ()))
contract_first = (((0,), (0,)), ((), ()))


def loop(count, step):
    if count <= 4:
        for i in range(count):
            step(i)
    else:
        pl.loop(0, count)(step)


def kernel(
    sizes, tok_hbm, go_hbm, routes_hbm, comb_hbm, wg_hbm, wu_hbm, wd_hbm,
    passed_ref, gc_ref, gg_ref, gu_ref, gd_ref,
    tok_ref, go_ref, routes_ref, comb_ref, stage, xg, wcat, packed, away, shares, shares_away,
    qbuf, hbuf, igsend, igrecv, ssend, srecv, fsend, frecv,
    isem, wsem, p1s, p1r, aws, gr, zs, qs, qr, igs, igr, ss, sr, fs, fr,
):
    pipes, E, DP, slices = sizes
    T = tok_ref.shape[1]
    top = routes_ref.shape[1]
    rows, hd = wg_hbm.shape[1:]
    pipe, e, d = (lax.axis_index(a) for a in ("pipe", "expert", "dp"))
    behind = lax.rem(pipe + pipes - 1, pipes)
    ahead = lax.rem(pipe + 1, pipes)
    my_expert = e // slices
    first, last_one = my_expert * slices, my_expert * slices + slices - 1
    experts = E // slices
    cap = min(T, max(2, 3 * T * top // (2 * experts)))
    slots = DP * cap
    pieces = 2 * slots // 16
    padded = DP * T

    def peer(r):
        return lax.rem(d + r, DP)

    def other(r):
        return lax.rem(e + r, E)

    barrier = pltpu.get_barrier_semaphore()

    def greet(*who):
        pl.semaphore_signal(barrier, inc=1, device_id=who, device_id_type=MESH)

    loop(DP - 1, lambda r: greet(pipe, e, peer(r + 1)))
    loop(E - 1, lambda r: greet(pipe, other(r + 1), d))
    loop(DP, lambda r: greet(ahead, e, r))

    given = [
        pltpu.make_async_copy(a, b, isem.at[i])
        for i, (a, b) in enumerate(
            (
                (routes_hbm, routes_ref), (comb_hbm, comb_ref),
                (tok_hbm, tok_ref), (go_hbm, go_ref),
            )
        )
    ]
    for c in given:
        c.start()
    loads = [
        pltpu.make_async_copy(w.at[0], wcat.at[:, pl.ds(i * hd, hd)], wsem.at[i])
        for i, w in enumerate((wg_hbm, wu_hbm, wd_hbm))
    ]
    for c in loads:
        c.start()

    lane = lax.broadcasted_iota(jnp.int32, (T, 128), 1)
    diagonal = lane == lax.broadcasted_iota(jnp.int32, (T, 128), 0)
    for c in given[:2]:
        c.wait()

    def column(row):
        spread = jnp.broadcast_to(row, (T, T))
        return jnp.sum(jnp.where(diagonal[:, :T], spread, 0), axis=1, keepdims=True)

    named = [column(routes_ref[0, k : k + 1, :]) for k in range(top)]
    weight = jnp.zeros((T, 128), F32)
    for k in range(top):
        share = column(comb_ref[0, k : k + 1, :].astype(F32))
        weight = weight + jnp.where(named[k] == lane, share, 0.0)
    for c in given[2:]:
        c.wait()
    tail = jnp.concatenate([weight, weight], axis=0).astype(BF16)
    for p in range(DP):
        both = jnp.concatenate(
            [
                tok_ref[0, :, p * rows : (p + 1) * rows].astype(F32),
                go_ref[0, :, p * rows : (p + 1) * rows].astype(F32),
            ],
            axis=0,
        ).astype(BF16)
        stage[p, :, :rows] = both
        stage[p, :, rows:] = tail

    pl.semaphore_wait(barrier, 2 * DP - 1 + E - 1)

    def remote(src, dst, send, recv, who):
        return pltpu.make_async_remote_copy(
            src_ref=src, dst_ref=dst, send_sem=send, recv_sem=recv,
            device_id=who, device_id_type=MESH,
        )

    def scatter(r):
        to = peer(r)
        return remote(stage.at[to], xg.at[d], p1s.at[r], p1r.at[d], (pipe, e, to))

    def scattered(r):
        p = peer(r)
        return remote(stage.at[p], xg.at[p], p1s.at[r], p1r.at[p], (pipe, e, p))

    def part(src, p):
        return shares.at[src] if p == pieces else packed.at[src, p]

    def send_away(j, p):
        to = jnp.where(j > my_expert, j * slices, j * slices + slices - 1)
        block = shares_away.at[j] if p == pieces else away.at[j, p]
        return remote(block, part(e, p), aws.at[j, p], gr.at[e, p], (pipe, to, d))

    def relay(src, p, way):
        block = part(src, p)
        to = jnp.clip(e + (1 if way == 0 else -1), 0, E - 1)
        return remote(block, block, zs.at[way, src, p], gr.at[src, p], (pipe, to, d))

    def going(src, way):
        if way == 0:
            return jnp.logical_and(src <= e, e < last_one)
        return jnp.logical_and(src >= e, e > first)

    def partial_to(src, r):
        block = qbuf.at[src * DP + d]
        return remote(block, block, qs.at[src, r], qr.at[src, d], (pipe, e, peer(r)))

    def partial_from(src, r):
        p = peer(r)
        block = qbuf.at[src * DP + p]
        return remote(block, block, qs.at[src, r], qr.at[src, p], (pipe, e, p))

    def rows_back(src):
        return remote(igsend.at[src], igrecv.at[e], igs.at[src], igr.at[e], (pipe, src, d))

    def score_back(src):
        return remote(ssend.at[src], srecv.at[e], ss.at[src], sr.at[e], (pipe, src, d))

    def rows_in(src):
        return remote(igsend.at[src], igrecv.at[src], igs.at[src], igr.at[src], (pipe, src, d))

    def score_in(src):
        return remote(ssend.at[src], srecv.at[src], ss.at[src], sr.at[src], (pipe, src, d))

    def hand_on(p):
        return remote(fsend.at[p], frecv.at[d], fs.at[p], fr.at[d], (behind, e, p))

    def handed(p):
        return remote(fsend.at[p], frecv.at[p], fs.at[p], fr.at[p], (behind, e, p))

    for r in range(1, DP):
        scatter(r).start()
    xg[d] = stage[d]

    count = DP * 2 * T
    at_row = lax.broadcasted_iota(jnp.int32, (count, 128), 0)
    at_lane = lax.broadcasted_iota(jnp.int32, (count, 128), 1)
    square_row = lax.broadcasted_iota(jnp.int32, (count, count), 0)
    square_col = lax.broadcasted_iota(jnp.int32, (count, count), 1)
    earlier = jnp.logical_and(square_row // T == square_col // T, square_col < square_row)
    base = (at_row // (2 * T)) * cap + (at_row // T) % 2 * slots
    for r in range(1, DP):
        scattered(r).wait_recv()
    plane = xg[...].reshape(count, rows + 128)
    plane_weight = plane[:, rows:].astype(F32)
    plane_rows = plane[:, :rows]
    here = jnp.where(plane_weight > 0.0, 1.0, 0.0)
    rank = jnp.dot(
        jnp.where(earlier, 1.0, 0.0).astype(BF16), here.astype(BF16), preferred_element_type=F32
    )
    slot = jnp.where(here > 0.0, base.astype(F32) + rank, -1.0)

    def pack(j):
        mine = at_lane == j
        to = jnp.sum(jnp.where(mine, slot, 0.0), axis=1, keepdims=True)
        share = jnp.sum(jnp.where(mine, plane_weight, 0.0), axis=1, keepdims=True)
        chosen = at_lane.astype(F32) == to
        row = jnp.sum(jnp.where(chosen, share, 0.0), axis=0, keepdims=True)
        onehot = jnp.where(chosen, 1.0, 0.0)[:, : 2 * slots].astype(BF16)
        moved = lax.dot_general(onehot, plane_rows, contract_first, preferred_element_type=F32)
        return moved.astype(BF16).reshape(pieces, 16, rows), jnp.broadcast_to(row, (8, 128))

    for k in range(1, experts):
        j = lax.rem(my_expert + k, experts)
        away[j], shares_away[j] = pack(j)
        for p in range(pieces + 1):
            send_away(j, p).start()
    packed[e], shares[e] = pack(my_expert)

    near = jnp.minimum(e, E - 1 - e)

    def source(i):
        half = (i + 1) // 2
        sign = jnp.where(i % 2 == 1, 1, -1)
        both_sides = e + sign * half
        one_side = jnp.where(e < E - 1 - e, e + (i - near), e - (i - near))
        return jnp.where(i <= 2 * near, both_sides, one_side)

    def arrive(i, own):
        src = e if own else source(i)
        for p in range(pieces + 1):
            if not own:
                relay(src, p, 0).wait_recv()
            for way in range(2):
                @pl.when(going(src, way))
                def _():
                    relay(src, p, way).start()
        return src

    def project(src):
        block = packed[src].reshape(2 * slots, rows)
        sums = jnp.dot(block, wcat[...], preferred_element_type=F32)
        q = jnp.concatenate([sums[:slots, : 2 * hd], sums[slots:, 2 * hd :]], axis=1)
        filler = jnp.zeros((padded - slots, 3 * hd), F32)
        qbuf[src * DP + d] = jnp.concatenate([q, filler], axis=0).astype(BF16)
        for r in range(1, DP):
            partial_to(src, r).start()

    def finish(src, own):
        for r in range(1, DP):
            partial_from(src, r).wait_recv()
        s = qbuf[src * DP].astype(F32)
        for p in range(1, DP):
            s = s + qbuf[src * DP + p].astype(F32)
        s = s[:slots]
        diag = at_lane[:slots] == at_row[:slots]
        g = jnp.sum(
            jnp.where(diag, jnp.broadcast_to(shares[src][:1], (slots, 128)), 0.0),
            axis=1, keepdims=True,
        )
        gate, up, hg = s[:, :hd], s[:, hd : 2 * hd], s[:, 2 * hd :]
        sig = jax.nn.sigmoid(gate)
        act = gate * sig
        hidden = (act * up).astype(BF16).astype(F32)
        hidden_grad = g * hg
        gate_grad = hidden_grad * up * sig * (1.0 + gate * (1.0 - sig))
        up_grad = hidden_grad * act
        score = jnp.sum(hidden * hg, axis=1, keepdims=True)
        score_row = jnp.sum(jnp.where(diag, score, 0.0), axis=0, keepdims=True)
        ssend[src] = jnp.broadcast_to(score_row, (8, 128))
        both = jnp.concatenate([gate_grad, up_grad], axis=1)
        upper = jnp.concatenate([both, jnp.zeros_like(gate)], axis=1)
        lower = jnp.concatenate([jnp.zeros_like(both), g * hidden], axis=1)
        hbuf[src] = jnp.concatenate([upper, lower], axis=0).astype(BF16)
        ig = lax.dot_general(
            both.astype(BF16), wcat[:, : 2 * hd], contract_last, preferred_element_type=F32
        )
        filler = jnp.zeros((padded - slots, rows), F32)
        ig = jnp.concatenate([ig, filler], axis=0).astype(BF16)
        if own:
            igrecv[src] = ig
            srecv[src] = ssend[src]
        else:
            igsend[src] = ig
            rows_back(src).start()
            score_back(src).start()

    src = arrive(0, True)
    for c in loads:
        c.wait()
    project(src)
    last = src
    if E <= 4:
        for i in range(1, E):
            src = arrive(i, False)
            project(src)
            finish(last, i == 1)
            last = src
        finish(last, False)
    else:
        finish(src, True)

        @pl.loop(1, E)
        def _(i):
            src = arrive(i, False)
            project(src)
            finish(src, False)

    if E <= 4:
        a = packed[...].reshape(E * 2 * slots, rows)
        b = hbuf[...].reshape(E * 2 * slots, 3 * hd)
        grads = lax.dot_general(a, b, contract_first, preferred_element_type=F32)
        for i, ref in enumerate((gg_ref, gu_ref, gd_ref)):
            ref[0] = grads[:, i * hd : (i + 1) * hd]
    else:
        for ref in (gg_ref, gu_ref, gd_ref):
            ref[0] = jnp.zeros((rows, hd), F32)

        @pl.loop(0, E)
        def _(j):
            a = packed[j].reshape(2 * slots, rows)
            b = hbuf[j]
            grads = lax.dot_general(a, b, contract_first, preferred_element_type=F32)
            for i, ref in enumerate((gg_ref, gu_ref, gd_ref)):
                ref[0] = ref[0] + grads[:, i * hd : (i + 1) * hd]

    def await_back(r):
        rows_in(other(r + 1)).wait_recv()
        score_in(other(r + 1)).wait_recv()

    loop(E - 1, await_back)
    group = 128 // padded

    def unpack(q):
        block = q * group + at_lane // padded
        place = jnp.zeros((count, 128), F32)
        for j in range(experts):
            hit = (at_lane % padded).astype(F32) == slot[:, j : j + 1]
            hit = jnp.logical_and(hit, at_lane % padded < slots)
            place = place + jnp.where(jnp.logical_and(hit, block // slices == j), 1.0, 0.0)
        got = igrecv[pl.ds(q * group, group)].reshape(128, rows)
        return jnp.dot(place.astype(BF16), got, preferred_element_type=F32)

    if E <= 4:
        total = unpack(0)
    else:
        total = lax.fori_loop(
            0, E // group, lambda q, t: t + unpack(q), jnp.zeros((count, rows), F32)
        )
    fsend[...] = total.reshape(DP, 2 * T, rows)[:, :T].astype(BF16)
    for p in range(DP):
        hand_on(p).start()

    tok_row = lax.broadcasted_iota(jnp.int32, (T, T), 0)
    tok_col = lax.broadcasted_iota(jnp.int32, (T, T), 1)
    tok_rank = jnp.dot(
        jnp.where(tok_col < tok_row, 1.0, 0.0).astype(BF16),
        jnp.where(weight > 0.0, 1.0, 0.0).astype(BF16),
        preferred_element_type=F32,
    )
    tok_slot = tok_rank + (d * cap).astype(F32)
    for k in range(top):
        own_slot = jnp.sum(jnp.where(named[k] == lane, tok_slot, 0.0), axis=1, keepdims=True)
        out = jnp.zeros((T, 1), F32)
        for j in range(E):
            if j % slices == 0:
                per = srecv[j]
                for m in range(1, slices):
                    per = per + srecv[j + m]
                pick = jnp.sum(
                    jnp.where(lane.astype(F32) == own_slot, per, 0.0), axis=1, keepdims=True
                )
                out = out + jnp.where(named[k] == j // slices, pick, 0.0)
        row = jnp.sum(jnp.where(diagonal, out, 0.0), axis=0, keepdims=True)
        gc_ref[0, k : k + 1, :] = row[:, :T]

    for r in range(1, DP):
        scatter(r).wait_send()

    for k in range(1, experts):
        for p in range(pieces + 1):
            send_away(lax.rem(my_expert + k, experts), p).wait_send()

    def sent(i):
        src = source(i)
        for p in range(pieces + 1):
            for way in range(2):
                @pl.when(going(src, way))
                def _():
                    relay(src, p, way).wait_send()
        for r in range(1, DP):
            partial_to(src, r).wait_send()

    loop(E, sent)

    def sent_back(r):
        rows_back(other(r + 1)).wait_send()
        score_back(other(r + 1)).wait_send()

    loop(E - 1, sent_back)
    for p in range(DP):
        handed(p).wait_recv()
        passed_ref[0, :, p * rows : (p + 1) * rows] = frecv[p]
    for p in range(DP):
        hand_on(p).wait_send()


def write_out(*refs):
    count = len(refs) // 2
    sems = refs[-1]
    copies = [
        pltpu.make_async_copy(refs[i], refs[count + i], sems.at[i]) for i in range(count)
    ]
    for c in copies:
        c.start()
    for c in copies:
        c.wait()


def solution(mesh):
    pipes, E, DP = (mesh.shape[a] for a in ("pipe", "expert", "dp"))
    slices = min(8, E // 2)

    def body(tokens, grad_out, routes, combine, w_gate, w_up, w_down):
        T, D = tokens.shape[1:]
        top = routes.shape[2]
        rows, hd = w_gate.shape[1:]
        experts = E // slices
        slots = DP * min(T, max(2, 3 * T * top // (2 * experts)))
        pieces = 2 * slots // 16
        vmem = pl.BlockSpec(memory_space=pltpu.VMEM)
        hbm = pl.BlockSpec(memory_space=pltpu.HBM)
        dma = pltpu.SemaphoreType.DMA
        grad = jax.ShapeDtypeStruct((1, rows, hd), F32)
        shapes = (
            jax.ShapeDtypeStruct((1, T, D), BF16),
            jax.ShapeDtypeStruct((1, top, T), F32),
            grad, grad, grad,
        )
        results = pl.pallas_call(
            functools.partial(kernel, (pipes, E, DP, slices)),
            out_shape=shapes,
            in_specs=[hbm] * 7,
            out_specs=[vmem] * 5,
            scratch_shapes=[
                pltpu.VMEM((1, T, D), BF16),
                pltpu.VMEM((1, T, D), BF16),
                pltpu.VMEM((1, top, T), jnp.int32),
                pltpu.VMEM((1, top, T), BF16),
                pltpu.VMEM((DP, 2 * T, rows + 128), BF16),
                pltpu.VMEM((DP, 2 * T, rows + 128), BF16),
                pltpu.VMEM((rows, 3 * hd), BF16),
                pltpu.VMEM((E, pieces, 16, rows), BF16),
                pltpu.VMEM((experts, pieces, 16, rows), BF16),
                pltpu.VMEM((E, 8, 128), F32),
                pltpu.VMEM((experts, 8, 128), F32),
                pltpu.VMEM((E * DP, DP * T, 3 * hd), BF16),
                pltpu.VMEM((E, 2 * slots, 3 * hd), BF16),
                pltpu.VMEM((E, DP * T, rows), BF16),
                pltpu.VMEM((E, DP * T, rows), BF16),
                pltpu.VMEM((E, 8, 128), F32),
                pltpu.VMEM((E, 8, 128), F32),
                pltpu.VMEM((DP, T, rows), BF16),
                pltpu.VMEM((DP, T, rows), BF16),
                dma((4,)), dma((3,)), dma((DP,)), dma((DP,)),
                dma((experts, pieces + 1)), dma((E, pieces + 1)), dma((2, E, pieces + 1)),
                dma((E, DP)), dma((E, DP)), dma((E,)), dma((E,)),
                dma((E,)), dma((E,)), dma((DP,)), dma((DP,)),
            ],
            compiler_params=pltpu.CompilerParams(
                collective_id=0, has_side_effects=True, vmem_limit_bytes=48 * 2**20
            ),
        )(
            *(
                pltpu.with_memory_space_constraint(a, pltpu.HBM)
                for a in (
                    tokens, grad_out, jnp.swapaxes(routes, 1, 2), jnp.swapaxes(combine, 1, 2),
                    w_gate, w_up, w_down,
                )
            )
        )
        passed, grad_combine, *grads = pl.pallas_call(
            write_out,
            out_shape=shapes,
            in_specs=[vmem] * 5,
            out_specs=[hbm] * 5,
            scratch_shapes=[dma((5,))],
            compiler_params=pltpu.CompilerParams(vmem_limit_bytes=2 * 2**20),
        )(*results)
        return (passed, jnp.swapaxes(grad_combine, 1, 2), *grads)

    weights = P("pipe", "dp", "expert")
    mine = P("pipe", ("expert", "dp"), None)
    return jax.shard_map(
        body, mesh=mesh, in_specs=(mine,) * 4 + (weights,) * 3,
        out_specs=(mine, mine, weights, weights, weights), check_vma=False,
    )
```

```python
import functools

import jax
import jax.numpy as jnp
from jax import lax
from jax.experimental import pallas as pl
from jax.experimental.pallas import tpu as pltpu
from jax.sharding import PartitionSpec as P

MESH = pl.DeviceIdType.MESH
F32, BF16 = jnp.float32, jnp.bfloat16
contract_last = (((1,), (1,)), ((), ()))
contract_first = (((0,), (0,)), ((), ()))


def loop(count, step):
    if count <= 4:
        for i in range(count):
            step(i)
    else:
        pl.loop(0, count)(step)


def kernel(
    sizes, tok_hbm, go_hbm, routes_hbm, comb_hbm, wg_hbm, wu_hbm, wd_hbm,
    passed_ref, gc_ref, gg_ref, gu_ref, gd_ref,
    routes_ref, comb_ref, xg, wbuf, wcat, qbuf, h_in, h_out, igsend, ssend, srecv, frecv,
    isem, wsem, p1s, ws, wr, gr, zs, qs, qr, igs, ss, sr, fr,
):
    pipes, E, DP, slices = sizes
    T = tok_hbm.shape[1]
    top = routes_ref.shape[1]
    rows, hd = wg_hbm.shape[1:]
    pipe, e, d = (lax.axis_index(a) for a in ("pipe", "expert", "dp"))
    behind = lax.rem(pipe + pipes - 1, pipes)
    ahead = lax.rem(pipe + 1, pipes)
    my_expert = e // slices

    def peer(r):
        return lax.rem(d + r, DP)

    def other(r):
        return lax.rem(e + r, E)

    barrier = pltpu.get_barrier_semaphore()

    def greet(*who):
        pl.semaphore_signal(barrier, inc=1, device_id=who, device_id_type=MESH)

    loop(DP - 1, lambda r: greet(pipe, e, peer(r + 1)))
    loop(E - 1, lambda r: greet(pipe, other(r + 1), d))
    loop(E, lambda j: loop(DP, lambda r: greet(ahead, j, r)))

    def mine(ref, p):
        return ref.at[0, :, pl.ds(pl.multiple_of(p * rows, rows), rows)]

    home = e * DP + d
    given = [
        pltpu.make_async_copy(a, b, isem.at[i])
        for i, (a, b) in enumerate(
            (
                (mine(tok_hbm, d), xg.at[home, 0]), (mine(go_hbm, d), xg.at[home, 1]),
                (routes_hbm, routes_ref), (comb_hbm, comb_ref),
            )
        )
    ]
    for c in given:
        c.start()
    loads = [
        pltpu.make_async_copy(w.at[0], wcat.at[:, pl.ds(i * hd, hd)], wsem.at[i])
        for i, w in enumerate((wg_hbm, wu_hbm, wd_hbm))
    ]
    for c in loads:
        c.start()

    pl.semaphore_wait(barrier, DP - 1 + E - 1 + E * DP)

    def remote(src, dst, send, recv, who):
        return pltpu.make_async_remote_copy(
            src_ref=src, dst_ref=dst, send_sem=send, recv_sem=recv,
            device_id=who, device_id_type=MESH,
        )

    def scatter(r, i):
        to = peer(r)
        ref = (tok_hbm, go_hbm)[i]
        return remote(mine(ref, to), xg.at[home, i], p1s.at[r, i], gr.at[e, d], (pipe, e, to))

    def part(src, p):
        return wbuf.at[src] if p == DP else xg.at[src * DP + p]

    def weights_to(r):
        block = wbuf.at[e, d]
        return remote(block, block, ws.at[r], wr.at[d], (pipe, e, peer(r)))

    def weights_from(r):
        p = peer(r)
        block = wbuf.at[e, p]
        return remote(block, block, ws.at[r], wr.at[p], (pipe, e, p))

    def relay(src, p, way):
        block = part(src, p) if isinstance(p, int) else xg.at[src * DP + p]
        to = jnp.clip(e + (1 if way == 0 else -1), 0, E - 1)
        return remote(block, block, zs.at[way, src, p], gr.at[src, p], (pipe, to, d))

    def going(src, way):
        if way == 0:
            return jnp.logical_and(src <= e, e + 1 < E)
        return jnp.logical_and(src >= e, e > 0)

    def partial_to(src, r):
        block = qbuf.at[src * DP + d]
        return remote(block, block, qs.at[src, r], qr.at[src, d], (pipe, e, peer(r)))

    def partial_from(src, r):
        p = peer(r)
        block = qbuf.at[src * DP + p]
        return remote(block, block, qs.at[src, r], qr.at[src, p], (pipe, e, p))

    def rows_back(src, p):
        return remote(
            igsend.at[src, p], frecv.at[e, d], igs.at[src, p], fr.at[e, d], (behind, src, p)
        )

    def rows_in(src, p):
        return remote(
            igsend.at[src, p], frecv.at[src, p], igs.at[src, p], fr.at[src, p], (behind, src, p)
        )

    def score_back(src):
        return remote(ssend.at[src, d], srecv.at[e], ss.at[src], sr.at[e], (pipe, src, d))

    def score_in(src):
        return remote(ssend.at[src, d], srecv.at[src], ss.at[src], sr.at[src], (pipe, src, d))

    for r in range(1, DP):
        for i in range(2):
            scatter(r, i).start()

    lane = lax.broadcasted_iota(jnp.int32, (T, 128), 1)
    diagonal = lane == lax.broadcasted_iota(jnp.int32, (T, 128), 0)
    for c in given[2:]:
        c.wait()

    def column(row):
        spread = jnp.broadcast_to(row, (T, T))
        return jnp.sum(jnp.where(diagonal[:, :T], spread, 0), axis=1, keepdims=True)

    named = [column(routes_ref[0, k : k + 1, :]) for k in range(top)]
    weight = jnp.zeros((T, 128), F32)
    for k in range(top):
        share = column(comb_ref[0, k : k + 1, :].astype(F32))
        weight = weight + jnp.where(named[k] == lane, share, 0.0)
    wbuf[e, d] = weight
    for r in range(1, DP):
        weights_to(r).start()
    for c in given[:2]:
        c.wait()

    near = jnp.minimum(e, E - 1 - e)

    def source(i):
        half = (i + 1) // 2
        sign = jnp.where(i % 2 == 1, 1, -1)
        both_sides = e + sign * half
        one_side = jnp.where(e < E - 1 - e, e + (i - near), e - (i - near))
        return jnp.where(i <= 2 * near, both_sides, one_side)

    def arrive(i, first):
        src = e if first else source(i)

        def pass_on(p):
            for way in range(2):
                @pl.when(going(src, way))
                def _():
                    relay(src, p, way).start()

        for r in range(DP):
            if not (first and r == 0):
                relay(src, peer(r), 0).wait_recv()
            pass_on(peer(r))
        if first:
            for r in range(1, DP):
                weights_from(r).wait_recv()
        else:
            relay(src, DP, 0).wait_recv()
        pass_on(DP)
        return src

    def sides(src):
        blocks = xg[pl.ds(src * DP, DP)]
        return [blocks[:, i].reshape(DP * T, rows) for i in range(2)]

    def project(src):
        x, out = sides(src)
        q = jnp.concatenate(
            [
                jnp.dot(x, wcat[:, : 2 * hd], preferred_element_type=F32),
                jnp.dot(out, wcat[:, 2 * hd :], preferred_element_type=F32),
            ],
            axis=1,
        )
        qbuf[src * DP + d] = q.astype(BF16)
        for r in range(1, DP):
            partial_to(src, r).start()

    def finish(src, own):
        for r in range(1, DP):
            partial_from(src, r).wait_recv()
        s = qbuf[src * DP].astype(F32)
        for p in range(1, DP):
            s = s + qbuf[src * DP + p].astype(F32)
        w = wbuf[src].reshape(DP * T, 128)
        at = lax.broadcasted_iota(jnp.int32, (DP * T, 128), 1)
        g = jnp.sum(jnp.where(at == my_expert, w, 0.0), axis=1, keepdims=True)
        gate, up, hg = s[:, :hd], s[:, hd : 2 * hd], s[:, 2 * hd :]
        sig = jax.nn.sigmoid(gate)
        act = gate * sig
        hidden = jnp.where(g > 0.0, (act * up).astype(BF16).astype(F32), 0.0)
        hidden_grad = g * hg
        gate_grad = hidden_grad * up * sig * (1.0 + gate * (1.0 - sig))
        up_grad = hidden_grad * act
        score = jnp.sum(hidden * hg, axis=1, keepdims=True)
        ssend[src] = jnp.broadcast_to(score, (DP * T, 128)).reshape(DP, T, 128)
        both = jnp.concatenate([gate_grad, up_grad], axis=1)
        h_in[src] = both.astype(BF16)
        h_out[src] = (g * hidden).astype(BF16)
        ig = lax.dot_general(
            both.astype(BF16), wcat[:, : 2 * hd], contract_last, preferred_element_type=F32
        ).astype(BF16)
        igsend[src] = ig.reshape(DP, T, rows)
        for p in range(DP):
            rows_back(src, p).start()
        if own:
            srecv[src] = ssend[src, d]
        else:
            score_back(src).start()

    src = arrive(0, True)
    for c in loads:
        c.wait()
    project(src)
    last = src
    if E <= 4:
        for i in range(1, E):
            src = arrive(i, False)
            project(src)
            finish(last, i == 1)
            last = src
        finish(last, False)
    else:
        finish(src, True)

        @pl.loop(1, E)
        def _(i):
            src = arrive(i, False)
            project(src)
            finish(src, False)

    if E <= 4:
        blocks = xg[...]
        x, out = [blocks[:, i].reshape(E * DP * T, rows) for i in range(2)]
        inward = lax.dot_general(
            x, h_in[...].reshape(E * DP * T, 2 * hd), contract_first, preferred_element_type=F32
        )
        gg_ref[0] = inward[:, :hd]
        gu_ref[0] = inward[:, hd:]
        gd_ref[0] = lax.dot_general(
            out, h_out[...].reshape(E * DP * T, hd), contract_first, preferred_element_type=F32
        )
    else:
        for ref in (gg_ref, gu_ref, gd_ref):
            ref[0] = jnp.zeros((rows, hd), F32)

        @pl.loop(0, E)
        def _(j):
            x, out = sides(j)
            inward = lax.dot_general(x, h_in[j], contract_first, preferred_element_type=F32)
            gg_ref[0] = gg_ref[0] + inward[:, :hd]
            gu_ref[0] = gu_ref[0] + inward[:, hd:]
            gd_ref[0] = gd_ref[0] + lax.dot_general(
                out, h_out[j], contract_first, preferred_element_type=F32
            )

    loop(E - 1, lambda r: score_in(other(r + 1)).wait_recv())
    for k in range(top):
        out = jnp.zeros((T, 128), F32)
        for j in range(E):
            if j % slices == 0:
                per = srecv[j]
                for m in range(1, slices):
                    per = per + srecv[j + m]
                out = out + jnp.where(named[k] == j // slices, per, 0.0)
        row = jnp.sum(jnp.where(diagonal, out, 0.0), axis=0, keepdims=True)
        gc_ref[0, k : k + 1, :] = row[:, :T]

    for r in range(1, DP):
        for i in range(2):
            scatter(r, i).wait_send()
        weights_to(r).wait_send()

    def sent(i):
        src = source(i)
        for p in [peer(r) for r in range(DP)] + [DP]:
            for way in range(2):
                @pl.when(going(src, way))
                def _():
                    relay(src, p, way).wait_send()
        for p in range(DP):
            rows_back(src, p).wait_send()
        for r in range(1, DP):
            partial_to(src, r).wait_send()

    loop(E, sent)

    loop(E - 1, lambda r: score_back(other(r + 1)).wait_send())

    loop(E, lambda j: loop(DP, lambda p: rows_in(j, p).wait_recv()))
    for p in range(DP):
        if E <= 4:
            total = frecv[0, p].astype(F32)
            for j in range(1, E):
                total = total + frecv[j, p].astype(F32)
        else:
            total = lax.fori_loop(
                0, E, lambda j, t: t + frecv[j, p].astype(F32), jnp.zeros((T, rows), F32)
            )
        passed_ref[0, :, p * rows : (p + 1) * rows] = total.astype(BF16)


def write_out(*refs):
    count = len(refs) // 2
    sems = refs[-1]
    copies = [
        pltpu.make_async_copy(refs[i], refs[count + i], sems.at[i]) for i in range(count)
    ]
    for c in copies:
        c.start()
    for c in copies:
        c.wait()


def solution(mesh):
    pipes, E, DP = (mesh.shape[a] for a in ("pipe", "expert", "dp"))
    slices = min(8, E // 2)

    def body(tokens, grad_out, routes, combine, w_gate, w_up, w_down):
        T, D = tokens.shape[1:]
        top = routes.shape[2]
        rows, hd = w_gate.shape[1:]
        vmem = pl.BlockSpec(memory_space=pltpu.VMEM)
        hbm = pl.BlockSpec(memory_space=pltpu.HBM)
        dma = pltpu.SemaphoreType.DMA
        grad = jax.ShapeDtypeStruct((1, rows, hd), F32)
        shapes = (
            jax.ShapeDtypeStruct((1, T, D), BF16),
            jax.ShapeDtypeStruct((1, top, T), F32),
            grad, grad, grad,
        )
        results = pl.pallas_call(
            functools.partial(kernel, (pipes, E, DP, slices)),
            out_shape=shapes,
            in_specs=[hbm] * 7,
            out_specs=[vmem] * 5,
            scratch_shapes=[
                pltpu.VMEM((1, top, T), jnp.int32),
                pltpu.VMEM((1, top, T), BF16),
                pltpu.VMEM((E * DP, 2, T, rows), BF16),
                pltpu.VMEM((E, DP, T, 128), F32),
                pltpu.VMEM((rows, 3 * hd), BF16),
                pltpu.VMEM((E * DP, DP * T, 3 * hd), BF16),
                pltpu.VMEM((E, DP * T, 2 * hd), BF16),
                pltpu.VMEM((E, DP * T, hd), BF16),
                pltpu.VMEM((E, DP, T, rows), BF16),
                pltpu.VMEM((E, DP, T, 128), F32),
                pltpu.VMEM((E, T, 128), F32),
                pltpu.VMEM((E, DP, T, rows), BF16),
                dma((4,)), dma((3,)), dma((DP, 2)), dma((DP,)), dma((DP,)),
                dma((E, DP + 1)), dma((2, E, DP + 1)), dma((E, DP)), dma((E, DP)),
                dma((E, DP)), dma((E,)), dma((E,)), dma((E, DP)),
            ],
            compiler_params=pltpu.CompilerParams(
                collective_id=0, has_side_effects=True, vmem_limit_bytes=48 * 2**20
            ),
        )(
            *(
                pltpu.with_memory_space_constraint(a, pltpu.HBM)
                for a in (
                    tokens, grad_out, jnp.swapaxes(routes, 1, 2), jnp.swapaxes(combine, 1, 2),
                    w_gate, w_up, w_down,
                )
            )
        )
        passed, grad_combine, *grads = pl.pallas_call(
            write_out,
            out_shape=shapes,
            in_specs=[vmem] * 5,
            out_specs=[hbm] * 5,
            scratch_shapes=[dma((5,))],
            compiler_params=pltpu.CompilerParams(vmem_limit_bytes=2 * 2**20),
        )(*results)
        return (passed, jnp.swapaxes(grad_combine, 1, 2), *grads)

    weights = P("pipe", "dp", "expert")
    mine = P("pipe", ("expert", "dp"), None)
    return jax.shard_map(
        body, mesh=mesh, in_specs=(mine,) * 4 + (weights,) * 3,
        out_specs=(mine, mine, weights, weights, weights), check_vma=False,
    )
```

```python
import functools

import jax
import jax.numpy as jnp
from jax import lax
from jax.experimental import pallas as pl
from jax.experimental.pallas import tpu as pltpu
from jax.sharding import PartitionSpec as P

MESH = pl.DeviceIdType.MESH
F32, BF16 = jnp.float32, jnp.bfloat16
contract_last = (((1,), (1,)), ((), ()))
contract_first = (((0,), (0,)), ((), ()))


def loop(count, step):
    if count <= 4:
        for i in range(count):
            step(i)
    else:
        pl.loop(0, count)(step)


def kernel(
    sizes, tok_hbm, go_hbm, routes_hbm, comb_hbm, wg_hbm, wu_hbm, wd_hbm,
    passed_ref, gc_ref, gg_ref, gu_ref, gd_ref,
    routes_ref, comb_ref, xg, wbuf, wcat, qbuf, h_in, h_out, igsend, ssend, srecv, frecv,
    isem, wsem, p1s, ws, wr, gr, zs, qs, qr, igs, ss, sr, fr,
):
    pipes, E, DP, slices = sizes
    T = tok_hbm.shape[1]
    top = routes_ref.shape[1]
    rows, hd = wg_hbm.shape[1:]
    pipe, e, d = (lax.axis_index(a) for a in ("pipe", "expert", "dp"))
    behind = lax.rem(pipe + pipes - 1, pipes)
    ahead = lax.rem(pipe + 1, pipes)
    my_expert = e // slices

    def peer(r):
        return lax.rem(d + r, DP)

    def other(r):
        return lax.rem(e + r, E)

    barrier = pltpu.get_barrier_semaphore()

    def greet(*who):
        pl.semaphore_signal(barrier, inc=1, device_id=who, device_id_type=MESH)

    loop(DP - 1, lambda r: greet(pipe, e, peer(r + 1)))
    loop(E - 1, lambda r: greet(pipe, other(r + 1), d))
    loop(E, lambda j: loop(DP, lambda r: greet(ahead, j, r)))

    def mine(ref, p):
        return ref.at[0, :, pl.ds(pl.multiple_of(p * rows, rows), rows)]

    home = e * DP + d
    given = [
        pltpu.make_async_copy(a, b, isem.at[i])
        for i, (a, b) in enumerate(
            (
                (mine(tok_hbm, d), xg.at[home, 0]), (mine(go_hbm, d), xg.at[home, 1]),
                (routes_hbm, routes_ref), (comb_hbm, comb_ref),
            )
        )
    ]
    for c in given:
        c.start()
    loads = [
        pltpu.make_async_copy(w.at[0], wcat.at[:, pl.ds(i * hd, hd)], wsem.at[i])
        for i, w in enumerate((wg_hbm, wu_hbm, wd_hbm))
    ]
    for c in loads:
        c.start()

    pl.semaphore_wait(barrier, DP - 1 + E - 1 + E * DP)

    def remote(src, dst, send, recv, who):
        return pltpu.make_async_remote_copy(
            src_ref=src, dst_ref=dst, send_sem=send, recv_sem=recv,
            device_id=who, device_id_type=MESH,
        )

    def scatter(r, i):
        to = peer(r)
        ref = (tok_hbm, go_hbm)[i]
        return remote(mine(ref, to), xg.at[home, i], p1s.at[r, i], gr.at[e, d], (pipe, e, to))

    def part(src, p):
        return wbuf.at[src] if p == DP else xg.at[src * DP + p]

    def weights_to(r):
        block = wbuf.at[e, d]
        return remote(block, block, ws.at[r], wr.at[d], (pipe, e, peer(r)))

    def weights_from(r):
        p = peer(r)
        block = wbuf.at[e, p]
        return remote(block, block, ws.at[r], wr.at[p], (pipe, e, p))

    def relay(src, p, way):
        block = part(src, p) if isinstance(p, int) else xg.at[src * DP + p]
        to = jnp.clip(e + (1 if way == 0 else -1), 0, E - 1)
        return remote(block, block, zs.at[way, src, p], gr.at[src, p], (pipe, to, d))

    def going(src, way):
        if way == 0:
            return jnp.logical_and(src <= e, e + 1 < E)
        return jnp.logical_and(src >= e, e > 0)

    def partial_to(src, r):
        block = qbuf.at[src * DP + d]
        return remote(block, block, qs.at[src, r], qr.at[src, d], (pipe, e, peer(r)))

    def partial_from(src, r):
        p = peer(r)
        block = qbuf.at[src * DP + p]
        return remote(block, block, qs.at[src, r], qr.at[src, p], (pipe, e, p))

    def rows_back(src, p):
        return remote(
            igsend.at[src, p], frecv.at[e, d], igs.at[src, p], fr.at[e, d], (behind, src, p)
        )

    def rows_in(src, p):
        return remote(
            igsend.at[src, p], frecv.at[src, p], igs.at[src, p], fr.at[src, p], (behind, src, p)
        )

    def score_back(src):
        return remote(ssend.at[src, d], srecv.at[e], ss.at[src], sr.at[e], (pipe, src, d))

    def score_in(src):
        return remote(ssend.at[src, d], srecv.at[src], ss.at[src], sr.at[src], (pipe, src, d))

    for r in range(1, DP):
        for i in range(2):
            scatter(r, i).start()

    lane = lax.broadcasted_iota(jnp.int32, (T, 128), 1)
    diagonal = lane == lax.broadcasted_iota(jnp.int32, (T, 128), 0)
    for c in given[2:]:
        c.wait()

    def column(row):
        spread = jnp.broadcast_to(row, (T, T))
        return jnp.sum(jnp.where(diagonal[:, :T], spread, 0), axis=1, keepdims=True)

    named = [column(routes_ref[0, k : k + 1, :]) for k in range(top)]
    weight = jnp.zeros((T, 128), F32)
    for k in range(top):
        share = column(comb_ref[0, k : k + 1, :].astype(F32))
        weight = weight + jnp.where(named[k] == lane, share, 0.0)
    wbuf[e, d] = weight
    for r in range(1, DP):
        weights_to(r).start()
    for c in given[:2]:
        c.wait()

    near = jnp.minimum(e, E - 1 - e)

    def source(i):
        half = (i + 1) // 2
        sign = jnp.where(i % 2 == 1, 1, -1) * jnp.where(2 * e < E, -1, 1)
        both_sides = e + sign * half
        one_side = jnp.where(e < E - 1 - e, e + (i - near), e - (i - near))
        return jnp.where(i <= 2 * near, both_sides, one_side)

    def arrive(i, first):
        src = e if first else source(i)

        def pass_on(p):
            for way in range(2):
                @pl.when(going(src, way))
                def _():
                    relay(src, p, way).start()

        for r in range(DP):
            if not (first and r == 0):
                relay(src, peer(r), 0).wait_recv()
            pass_on(peer(r))
        if first:
            for r in range(1, DP):
                weights_from(r).wait_recv()
        else:
            relay(src, DP, 0).wait_recv()
        pass_on(DP)
        return src

    def sides(src):
        blocks = xg[pl.ds(src * DP, DP)]
        return [blocks[:, i].reshape(DP * T, rows) for i in range(2)]

    def project(src):
        x, out = sides(src)
        q = jnp.concatenate(
            [
                jnp.dot(x, wcat[:, : 2 * hd], preferred_element_type=F32),
                jnp.dot(out, wcat[:, 2 * hd :], preferred_element_type=F32),
            ],
            axis=1,
        )
        qbuf[src * DP + d] = q.astype(BF16)
        for r in range(1, DP):
            partial_to(src, r).start()

    def finish(src, own):
        for r in range(1, DP):
            partial_from(src, r).wait_recv()
        s = qbuf[src * DP].astype(F32)
        for p in range(1, DP):
            s = s + qbuf[src * DP + p].astype(F32)
        w = wbuf[src].reshape(DP * T, 128)
        at = lax.broadcasted_iota(jnp.int32, (DP * T, 128), 1)
        g = jnp.sum(jnp.where(at == my_expert, w, 0.0), axis=1, keepdims=True)
        gate, up, hg = s[:, :hd], s[:, hd : 2 * hd], s[:, 2 * hd :]
        sig = jax.nn.sigmoid(gate)
        act = gate * sig
        hidden = jnp.where(g > 0.0, (act * up).astype(BF16).astype(F32), 0.0)
        hidden_grad = g * hg
        gate_grad = hidden_grad * up * sig * (1.0 + gate * (1.0 - sig))
        up_grad = hidden_grad * act
        score = jnp.sum(hidden * hg, axis=1, keepdims=True)
        ssend[src] = jnp.broadcast_to(score, (DP * T, 128)).reshape(DP, T, 128)
        both = jnp.concatenate([gate_grad, up_grad], axis=1)
        h_in[src] = both.astype(BF16)
        h_out[src] = (g * hidden).astype(BF16)
        ig = lax.dot_general(
            both.astype(BF16), wcat[:, : 2 * hd], contract_last, preferred_element_type=F32
        ).astype(BF16)
        igsend[src] = ig.reshape(DP, T, rows)
        for p in range(DP):
            rows_back(src, p).start()
        if own:
            srecv[src] = ssend[src, d]
        else:
            score_back(src).start()

    src = arrive(0, True)
    for c in loads:
        c.wait()
    project(src)
    if E <= 4:
        near_by, far = range(1, min(E, 3)), range(3, E)
        planes = [arrive(i, False) for i in near_by]
        for plane in planes:
            project(plane)
        finish(src, True)
        for i in far:
            planes.append(arrive(i, False))
            project(planes[-1])
        for plane in planes:
            finish(plane, False)
    else:
        finish(src, True)

        @pl.loop(1, E)
        def _(i):
            src = arrive(i, False)
            project(src)
            finish(src, False)

    if E <= 4:
        blocks = xg[...]
        x, out = [blocks[:, i].reshape(E * DP * T, rows) for i in range(2)]
        inward = lax.dot_general(
            x, h_in[...].reshape(E * DP * T, 2 * hd), contract_first, preferred_element_type=F32
        )
        gg_ref[0] = inward[:, :hd]
        gu_ref[0] = inward[:, hd:]
        gd_ref[0] = lax.dot_general(
            out, h_out[...].reshape(E * DP * T, hd), contract_first, preferred_element_type=F32
        )
    else:
        for ref in (gg_ref, gu_ref, gd_ref):
            ref[0] = jnp.zeros((rows, hd), F32)

        @pl.loop(0, E)
        def _(j):
            x, out = sides(j)
            inward = lax.dot_general(x, h_in[j], contract_first, preferred_element_type=F32)
            gg_ref[0] = gg_ref[0] + inward[:, :hd]
            gu_ref[0] = gu_ref[0] + inward[:, hd:]
            gd_ref[0] = gd_ref[0] + lax.dot_general(
                out, h_out[j], contract_first, preferred_element_type=F32
            )

    loop(E - 1, lambda r: score_in(other(r + 1)).wait_recv())
    for k in range(top):
        out = jnp.zeros((T, 128), F32)
        for j in range(E):
            if j % slices == 0:
                per = srecv[j]
                for m in range(1, slices):
                    per = per + srecv[j + m]
                out = out + jnp.where(named[k] == j // slices, per, 0.0)
        row = jnp.sum(jnp.where(diagonal, out, 0.0), axis=0, keepdims=True)
        gc_ref[0, k : k + 1, :] = row[:, :T]

    for r in range(1, DP):
        for i in range(2):
            scatter(r, i).wait_send()
        weights_to(r).wait_send()

    def sent(i):
        src = source(i)
        for p in [peer(r) for r in range(DP)] + [DP]:
            for way in range(2):
                @pl.when(going(src, way))
                def _():
                    relay(src, p, way).wait_send()
        for p in range(DP):
            rows_back(src, p).wait_send()
        for r in range(1, DP):
            partial_to(src, r).wait_send()

    loop(E, sent)

    loop(E - 1, lambda r: score_back(other(r + 1)).wait_send())

    loop(E, lambda j: loop(DP, lambda p: rows_in(j, p).wait_recv()))
    for p in range(DP):
        if E <= 4:
            total = frecv[0, p].astype(F32)
            for j in range(1, E):
                total = total + frecv[j, p].astype(F32)
        else:
            total = lax.fori_loop(
                0, E, lambda j, t: t + frecv[j, p].astype(F32), jnp.zeros((T, rows), F32)
            )
        passed_ref[0, :, p * rows : (p + 1) * rows] = total.astype(BF16)


def write_out(*refs):
    count = len(refs) // 2
    sems = refs[-1]
    copies = [
        pltpu.make_async_copy(refs[i], refs[count + i], sems.at[i]) for i in range(count)
    ]
    for c in copies:
        c.start()
    for c in copies:
        c.wait()


def solution(mesh):
    pipes, E, DP = (mesh.shape[a] for a in ("pipe", "expert", "dp"))
    slices = min(8, E // 2)

    def body(tokens, grad_out, routes, combine, w_gate, w_up, w_down):
        T, D = tokens.shape[1:]
        top = routes.shape[2]
        rows, hd = w_gate.shape[1:]
        vmem = pl.BlockSpec(memory_space=pltpu.VMEM)
        hbm = pl.BlockSpec(memory_space=pltpu.HBM)
        dma = pltpu.SemaphoreType.DMA
        grad = jax.ShapeDtypeStruct((1, rows, hd), F32)
        shapes = (
            jax.ShapeDtypeStruct((1, T, D), BF16),
            jax.ShapeDtypeStruct((1, top, T), F32),
            grad, grad, grad,
        )
        results = pl.pallas_call(
            functools.partial(kernel, (pipes, E, DP, slices)),
            out_shape=shapes,
            in_specs=[hbm] * 7,
            out_specs=[vmem] * 5,
            scratch_shapes=[
                pltpu.VMEM((1, top, T), jnp.int32),
                pltpu.VMEM((1, top, T), BF16),
                pltpu.VMEM((E * DP, 2, T, rows), BF16),
                pltpu.VMEM((E, DP, T, 128), F32),
                pltpu.VMEM((rows, 3 * hd), BF16),
                pltpu.VMEM((E * DP, DP * T, 3 * hd), BF16),
                pltpu.VMEM((E, DP * T, 2 * hd), BF16),
                pltpu.VMEM((E, DP * T, hd), BF16),
                pltpu.VMEM((E, DP, T, rows), BF16),
                pltpu.VMEM((E, DP, T, 128), F32),
                pltpu.VMEM((E, T, 128), F32),
                pltpu.VMEM((E, DP, T, rows), BF16),
                dma((4,)), dma((3,)), dma((DP, 2)), dma((DP,)), dma((DP,)),
                dma((E, DP + 1)), dma((2, E, DP + 1)), dma((E, DP)), dma((E, DP)),
                dma((E, DP)), dma((E,)), dma((E,)), dma((E, DP)),
            ],
            compiler_params=pltpu.CompilerParams(
                collective_id=0, has_side_effects=True, vmem_limit_bytes=48 * 2**20
            ),
        )(
            *(
                pltpu.with_memory_space_constraint(a, pltpu.HBM)
                for a in (
                    tokens, grad_out, jnp.swapaxes(routes, 1, 2), jnp.swapaxes(combine, 1, 2),
                    w_gate, w_up, w_down,
                )
            )
        )
        passed, grad_combine, *grads = pl.pallas_call(
            write_out,
            out_shape=shapes,
            in_specs=[vmem] * 5,
            out_specs=[hbm] * 5,
            scratch_shapes=[dma((5,))],
            compiler_params=pltpu.CompilerParams(vmem_limit_bytes=2 * 2**20),
        )(*results)
        return (passed, jnp.swapaxes(grad_combine, 1, 2), *grads)

    weights = P("pipe", "dp", "expert")
    mine = P("pipe", ("expert", "dp"), None)
    return jax.shard_map(
        body, mesh=mesh, in_specs=(mine,) * 4 + (weights,) * 3,
        out_specs=(mine, mine, weights, weights, weights), check_vma=False,
    )
```

```python
import functools

import jax
import jax.numpy as jnp
from jax import lax
from jax.experimental import pallas as pl
from jax.experimental.pallas import tpu as pltpu
from jax.sharding import PartitionSpec as P

MESH = pl.DeviceIdType.MESH
F32, BF16 = jnp.float32, jnp.bfloat16
contract_first = (((0,), (0,)), ((), ()))


def loop(count, step):
    if count <= 4:
        for i in range(count):
            step(i)
    else:
        pl.loop(0, count)(step)


def kernel(
    sizes, tok_hbm, go_hbm, routes_hbm, comb_hbm, wg_hbm, wu_hbm, wd_hbm,
    passed_ref, gc_ref, gg_ref, gu_ref, gd_ref,
    routes_ref, comb_ref, xg, wbuf, wcat, flipped, qbuf, h_in, h_out, igsend, ssend, srecv, frecv,
    isem, wsem, p1s, ws, wr, gr, zs, qs, qr, igs, ss, sr, fr,
):
    pipes, E, DP, slices = sizes
    T = tok_hbm.shape[1]
    top = routes_ref.shape[1]
    rows, hd = wg_hbm.shape[1:]
    pipe, e, d = (lax.axis_index(a) for a in ("pipe", "expert", "dp"))
    behind = lax.rem(pipe + pipes - 1, pipes)
    ahead = lax.rem(pipe + 1, pipes)
    my_expert = e // slices

    def peer(r):
        return lax.rem(d + r, DP)

    def other(r):
        return lax.rem(e + r, E)

    barrier = pltpu.get_barrier_semaphore()

    def greet(*who):
        pl.semaphore_signal(barrier, inc=1, device_id=who, device_id_type=MESH)

    loop(DP - 1, lambda r: greet(pipe, e, peer(r + 1)))
    loop(E - 1, lambda r: greet(pipe, other(r + 1), d))
    loop(E, lambda j: loop(DP, lambda r: greet(ahead, j, r)))

    def mine(ref, p):
        return ref.at[0, :, pl.ds(pl.multiple_of(p * rows, rows), rows)]

    home = e * DP + d
    given = [
        pltpu.make_async_copy(a, b, isem.at[i])
        for i, (a, b) in enumerate(
            (
                (mine(tok_hbm, d), xg.at[home, 0]), (mine(go_hbm, d), xg.at[home, 1]),
                (routes_hbm, routes_ref), (comb_hbm, comb_ref),
            )
        )
    ]
    for c in given:
        c.start()
    loads = [
        pltpu.make_async_copy(w.at[0], wcat.at[:, pl.ds(i * hd, hd)], wsem.at[i])
        for i, w in enumerate((wg_hbm, wu_hbm, wd_hbm))
    ]
    for c in loads:
        c.start()

    pl.semaphore_wait(barrier, DP - 1 + E - 1 + E * DP)

    def remote(src, dst, send, recv, who):
        return pltpu.make_async_remote_copy(
            src_ref=src, dst_ref=dst, send_sem=send, recv_sem=recv,
            device_id=who, device_id_type=MESH,
        )

    def scatter(r, i):
        to = peer(r)
        ref = (tok_hbm, go_hbm)[i]
        return remote(mine(ref, to), xg.at[home, i], p1s.at[r, i], gr.at[e, d], (pipe, e, to))

    def part(src, p):
        return wbuf.at[src] if p == DP else xg.at[src * DP + p]

    def weights_to(r):
        block = wbuf.at[e, d]
        return remote(block, block, ws.at[r], wr.at[d], (pipe, e, peer(r)))

    def weights_from(r):
        p = peer(r)
        block = wbuf.at[e, p]
        return remote(block, block, ws.at[r], wr.at[p], (pipe, e, p))

    def give(p, to):
        block = part(e, p) if isinstance(p, int) else xg.at[e * DP + p]
        return remote(block, block, zs.at[to, p], gr.at[e, p], (pipe, to, d))

    def shared(src, p):
        block = part(src, p) if isinstance(p, int) else xg.at[src * DP + p]
        return remote(block, block, zs.at[src, p], gr.at[src, p], (pipe, src, d))

    def partial_to(src, r):
        block = qbuf.at[src * DP + d]
        return remote(block, block, qs.at[src, r], qr.at[src, d], (pipe, e, peer(r)))

    def partial_from(src, r):
        p = peer(r)
        block = qbuf.at[src * DP + p]
        return remote(block, block, qs.at[src, r], qr.at[src, p], (pipe, e, p))

    def rows_back(src, p):
        return remote(
            igsend.at[src, p], frecv.at[e, d], igs.at[src, p], fr.at[e, d], (behind, src, p)
        )

    def rows_in(src, p):
        return remote(
            igsend.at[src, p], frecv.at[src, p], igs.at[src, p], fr.at[src, p], (behind, src, p)
        )

    def score_back(src):
        return remote(ssend.at[src, d], srecv.at[e], ss.at[src], sr.at[e], (pipe, src, d))

    def score_in(src):
        return remote(ssend.at[src, d], srecv.at[src], ss.at[src], sr.at[src], (pipe, src, d))

    for r in range(1, DP):
        for i in range(2):
            scatter(r, i).start()

    lane = lax.broadcasted_iota(jnp.int32, (T, 128), 1)
    diagonal = lane == lax.broadcasted_iota(jnp.int32, (T, 128), 0)
    for c in given[2:]:
        c.wait()

    def column(row):
        spread = jnp.broadcast_to(row, (T, T))
        return jnp.sum(jnp.where(diagonal[:, :T], spread, 0), axis=1, keepdims=True)

    named = [column(routes_ref[0, k : k + 1, :]) for k in range(top)]
    weight = jnp.zeros((T, 128), F32)
    for k in range(top):
        share = column(comb_ref[0, k : k + 1, :].astype(F32))
        weight = weight + jnp.where(named[k] == lane, share, 0.0)
    wbuf[e, d] = weight
    for r in range(1, DP):
        weights_to(r).start()
    for c in given[:2]:
        c.wait()

    near = jnp.minimum(e, E - 1 - e)

    def source(i):
        half = (i + 1) // 2
        sign = jnp.where(i % 2 == 1, 1, -1) * jnp.where(2 * e < E, -1, 1)
        both_sides = e + sign * half
        one_side = jnp.where(e < E - 1 - e, e + (i - near), e - (i - near))
        return jnp.where(i <= 2 * near, both_sides, one_side)

    def arrive(i, first):
        src = e if first else source(i)

        def pass_on(p):
            if first:
                loop(E - 1, lambda r: give(p, other(r + 1)).start())

        for r in range(DP):
            if not (first and r == 0):
                shared(src, peer(r)).wait_recv()
            pass_on(peer(r))
        if first:
            for r in range(1, DP):
                weights_from(r).wait_recv()
        else:
            shared(src, DP).wait_recv()
        pass_on(DP)
        return src

    def sides(src):
        blocks = xg[pl.ds(src * DP, DP)]
        return [blocks[:, i].reshape(DP * T, rows) for i in range(2)]

    def project(src):
        x, out = sides(src)
        q = jnp.concatenate(
            [
                jnp.dot(x, wcat[:, : 2 * hd], preferred_element_type=F32),
                jnp.dot(out, wcat[:, 2 * hd :], preferred_element_type=F32),
            ],
            axis=1,
        )
        qbuf[src * DP + d] = q.astype(BF16)
        for r in range(1, DP):
            partial_to(src, r).start()

    def finish(src, own):
        for r in range(1, DP):
            partial_from(src, r).wait_recv()
        s = qbuf[src * DP].astype(F32)
        for p in range(1, DP):
            s = s + qbuf[src * DP + p].astype(F32)
        w = wbuf[src].reshape(DP * T, 128)
        at = lax.broadcasted_iota(jnp.int32, (DP * T, 128), 1)
        g = jnp.sum(jnp.where(at == my_expert, w, 0.0), axis=1, keepdims=True)
        gate, up, hg = s[:, :hd], s[:, hd : 2 * hd], s[:, 2 * hd :]
        sig = jax.nn.sigmoid(gate)
        act = gate * sig
        hidden = jnp.where(g > 0.0, (act * up).astype(BF16).astype(F32), 0.0)
        hidden_grad = g * hg
        gate_grad = hidden_grad * up * sig * (1.0 + gate * (1.0 - sig))
        up_grad = hidden_grad * act
        score = jnp.sum(hidden * hg, axis=1, keepdims=True)
        ssend[src] = jnp.broadcast_to(score, (DP * T, 128)).reshape(DP, T, 128)
        both = jnp.concatenate([gate_grad, up_grad], axis=1)
        h_in[src] = both.astype(BF16)
        h_out[src] = (g * hidden).astype(BF16)
        ig = jnp.dot(
            both.astype(BF16), flipped[...], preferred_element_type=F32
        ).astype(BF16)
        igsend[src] = ig.reshape(DP, T, rows)
        for p in range(DP):
            rows_back(src, p).start()
        if own:
            srecv[src] = ssend[src, d]
        else:
            score_back(src).start()

    for c in loads:
        c.wait()
    flipped[...] = wcat[:, : 2 * hd].T
    src = arrive(0, True)
    project(src)
    if E <= 4:
        near_by, far = range(1, min(E, 3)), range(3, E)
        planes = [arrive(i, False) for i in near_by]
        for plane in planes:
            project(plane)
        finish(src, True)
        for i in far:
            planes.append(arrive(i, False))
            project(planes[-1])
        for plane in planes:
            finish(plane, False)
    else:
        finish(src, True)

        @pl.loop(1, E)
        def _(i):
            src = arrive(i, False)
            project(src)
            finish(src, False)

    if E <= 4:
        blocks = xg[...]
        x, out = [blocks[:, i].reshape(E * DP * T, rows) for i in range(2)]
        inward = lax.dot_general(
            x, h_in[...].reshape(E * DP * T, 2 * hd), contract_first, preferred_element_type=F32
        )
        gg_ref[0] = inward[:, :hd]
        gu_ref[0] = inward[:, hd:]
        gd_ref[0] = lax.dot_general(
            out, h_out[...].reshape(E * DP * T, hd), contract_first, preferred_element_type=F32
        )
    else:
        for ref in (gg_ref, gu_ref, gd_ref):
            ref[0] = jnp.zeros((rows, hd), F32)

        @pl.loop(0, E)
        def _(j):
            x, out = sides(j)
            inward = lax.dot_general(x, h_in[j], contract_first, preferred_element_type=F32)
            gg_ref[0] = gg_ref[0] + inward[:, :hd]
            gu_ref[0] = gu_ref[0] + inward[:, hd:]
            gd_ref[0] = gd_ref[0] + lax.dot_general(
                out, h_out[j], contract_first, preferred_element_type=F32
            )

    loop(E - 1, lambda r: score_in(other(r + 1)).wait_recv())
    for k in range(top):
        out = jnp.zeros((T, 128), F32)
        for j in range(E):
            if j % slices == 0:
                per = srecv[j]
                for m in range(1, slices):
                    per = per + srecv[j + m]
                out = out + jnp.where(named[k] == j // slices, per, 0.0)
        row = jnp.sum(jnp.where(diagonal, out, 0.0), axis=0, keepdims=True)
        gc_ref[0, k : k + 1, :] = row[:, :T]

    for r in range(1, DP):
        for i in range(2):
            scatter(r, i).wait_send()
        weights_to(r).wait_send()

    def sent(i):
        src = source(i)
        for p in range(DP):
            rows_back(src, p).wait_send()
        for r in range(1, DP):
            partial_to(src, r).wait_send()

    loop(E, sent)
    for p in [peer(r) for r in range(DP)] + [DP]:
        loop(E - 1, lambda r: give(p, other(r + 1)).wait_send())

    loop(E - 1, lambda r: score_back(other(r + 1)).wait_send())

    loop(E, lambda j: loop(DP, lambda p: rows_in(j, p).wait_recv()))
    for p in range(DP):
        if E <= 4:
            total = frecv[0, p].astype(F32)
            for j in range(1, E):
                total = total + frecv[j, p].astype(F32)
        else:
            total = lax.fori_loop(
                0, E, lambda j, t: t + frecv[j, p].astype(F32), jnp.zeros((T, rows), F32)
            )
        passed_ref[0, :, p * rows : (p + 1) * rows] = total.astype(BF16)


def write_out(*refs):
    count = len(refs) // 2
    sems = refs[-1]
    copies = [
        pltpu.make_async_copy(refs[i], refs[count + i], sems.at[i]) for i in range(count)
    ]
    for c in copies:
        c.start()
    for c in copies:
        c.wait()


def solution(mesh):
    pipes, E, DP = (mesh.shape[a] for a in ("pipe", "expert", "dp"))
    slices = min(8, E // 2)

    def body(tokens, grad_out, routes, combine, w_gate, w_up, w_down):
        T, D = tokens.shape[1:]
        top = routes.shape[2]
        rows, hd = w_gate.shape[1:]
        vmem = pl.BlockSpec(memory_space=pltpu.VMEM)
        hbm = pl.BlockSpec(memory_space=pltpu.HBM)
        dma = pltpu.SemaphoreType.DMA
        grad = jax.ShapeDtypeStruct((1, rows, hd), F32)
        shapes = (
            jax.ShapeDtypeStruct((1, T, D), BF16),
            jax.ShapeDtypeStruct((1, top, T), F32),
            grad, grad, grad,
        )
        results = pl.pallas_call(
            functools.partial(kernel, (pipes, E, DP, slices)),
            out_shape=shapes,
            in_specs=[hbm] * 7,
            out_specs=[vmem] * 5,
            scratch_shapes=[
                pltpu.VMEM((1, top, T), jnp.int32),
                pltpu.VMEM((1, top, T), BF16),
                pltpu.VMEM((E * DP, 2, T, rows), BF16),
                pltpu.VMEM((E, DP, T, 128), F32),
                pltpu.VMEM((rows, 3 * hd), BF16),
                pltpu.VMEM((2 * hd, rows), BF16),
                pltpu.VMEM((E * DP, DP * T, 3 * hd), BF16),
                pltpu.VMEM((E, DP * T, 2 * hd), BF16),
                pltpu.VMEM((E, DP * T, hd), BF16),
                pltpu.VMEM((E, DP, T, rows), BF16),
                pltpu.VMEM((E, DP, T, 128), F32),
                pltpu.VMEM((E, T, 128), F32),
                pltpu.VMEM((E, DP, T, rows), BF16),
                dma((4,)), dma((3,)), dma((DP, 2)), dma((DP,)), dma((DP,)),
                dma((E, DP + 1)), dma((E, DP + 1)), dma((E, DP)), dma((E, DP)),
                dma((E, DP)), dma((E,)), dma((E,)), dma((E, DP)),
            ],
            compiler_params=pltpu.CompilerParams(
                collective_id=0, has_side_effects=True, vmem_limit_bytes=48 * 2**20
            ),
        )(
            *(
                pltpu.with_memory_space_constraint(a, pltpu.HBM)
                for a in (
                    tokens, grad_out, jnp.swapaxes(routes, 1, 2), jnp.swapaxes(combine, 1, 2),
                    w_gate, w_up, w_down,
                )
            )
        )
        passed, grad_combine, *grads = pl.pallas_call(
            write_out,
            out_shape=shapes,
            in_specs=[vmem] * 5,
            out_specs=[hbm] * 5,
            scratch_shapes=[dma((5,))],
            compiler_params=pltpu.CompilerParams(vmem_limit_bytes=2 * 2**20),
        )(*results)
        return (passed, jnp.swapaxes(grad_combine, 1, 2), *grads)

    weights = P("pipe", "dp", "expert")
    mine = P("pipe", ("expert", "dp"), None)
    return jax.shard_map(
        body, mesh=mesh, in_specs=(mine,) * 4 + (weights,) * 3,
        out_specs=(mine, mine, weights, weights, weights), check_vma=False,
    )
```

```python
import functools

import jax
import jax.numpy as jnp
from jax import lax
from jax.experimental import pallas as pl
from jax.experimental.pallas import tpu as pltpu
from jax.sharding import PartitionSpec as P

MESH = pl.DeviceIdType.MESH
F32, BF16 = jnp.float32, jnp.bfloat16
contract_first = (((0,), (0,)), ((), ()))


def loop(count, step):
    if count <= 4:
        for i in range(count):
            step(i)
    else:
        pl.loop(0, count)(step)


def kernel(
    sizes, tok_hbm, go_hbm, routes_hbm, comb_hbm, wg_hbm, wu_hbm, wd_hbm,
    passed_ref, gc_ref, gg_ref, gu_ref, gd_ref,
    routes_ref, comb_ref, xg, wbuf, wcat, flipped, qbuf, h_in, h_out, igsend, ssend, srecv, frecv,
    isem, wsem, p1s, ws, wr, gr, zs, qs, qr, igs, ss, sr, fr,
):
    pipes, E, DP, slices = sizes
    T = tok_hbm.shape[1]
    top = routes_ref.shape[1]
    rows, hd = wg_hbm.shape[1:]
    pipe, e, d = (lax.axis_index(a) for a in ("pipe", "expert", "dp"))
    behind = lax.rem(pipe + pipes - 1, pipes)
    ahead = lax.rem(pipe + 1, pipes)
    my_expert = e // slices

    def peer(r):
        return lax.rem(d + r, DP)

    def other(r):
        return lax.rem(e + r, E)

    barrier = pltpu.get_barrier_semaphore()

    def greet(*who):
        pl.semaphore_signal(barrier, inc=1, device_id=who, device_id_type=MESH)

    loop(DP - 1, lambda r: greet(pipe, e, peer(r + 1)))
    loop(E - 1, lambda r: greet(pipe, other(r + 1), d))
    loop(E, lambda j: loop(DP, lambda r: greet(ahead, j, r)))

    def mine(ref, p):
        return ref.at[0, :, pl.ds(pl.multiple_of(p * rows, rows), rows)]

    home = e * DP + d
    given = [
        pltpu.make_async_copy(a, b, isem.at[i])
        for i, (a, b) in enumerate(
            (
                (mine(tok_hbm, d), xg.at[home, 0]), (mine(go_hbm, d), xg.at[home, 1]),
                (routes_hbm, routes_ref), (comb_hbm, comb_ref),
            )
        )
    ]
    for c in given:
        c.start()
    loads = [
        pltpu.make_async_copy(w.at[0], wcat.at[:, pl.ds(i * hd, hd)], wsem.at[i])
        for i, w in enumerate((wg_hbm, wu_hbm, wd_hbm))
    ]
    for c in loads:
        c.start()

    pl.semaphore_wait(barrier, DP - 1 + E - 1 + E * DP)

    def remote(src, dst, send, recv, who):
        return pltpu.make_async_remote_copy(
            src_ref=src, dst_ref=dst, send_sem=send, recv_sem=recv,
            device_id=who, device_id_type=MESH,
        )

    def scatter(r, i):
        to = peer(r)
        ref = (tok_hbm, go_hbm)[i]
        return remote(mine(ref, to), xg.at[home, i], p1s.at[r, i], gr.at[e, d], (pipe, e, to))

    def part(src, p):
        return wbuf.at[src] if p == DP else xg.at[src * DP + p]

    def weights_to(r):
        block = wbuf.at[e, d]
        return remote(block, block, ws.at[r], wr.at[d], (pipe, e, peer(r)))

    def weights_from(r):
        p = peer(r)
        block = wbuf.at[e, p]
        return remote(block, block, ws.at[r], wr.at[p], (pipe, e, p))

    def relay(src, p, way):
        block = part(src, p) if isinstance(p, int) else xg.at[src * DP + p]
        to = jnp.clip(e + (1 if way == 0 else -1), 0, E - 1)
        return remote(block, block, zs.at[way, src, p], gr.at[src, p], (pipe, to, d))

    def going(src, way):
        if way == 0:
            return jnp.logical_and(src <= e, e + 1 < E)
        return jnp.logical_and(src >= e, e > 0)

    def partial_to(src, r):
        block = qbuf.at[src * DP + d]
        return remote(block, block, qs.at[src, r], qr.at[src, d], (pipe, e, peer(r)))

    def partial_from(src, r):
        p = peer(r)
        block = qbuf.at[src * DP + p]
        return remote(block, block, qs.at[src, r], qr.at[src, p], (pipe, e, p))

    def rows_back(src, p):
        return remote(
            igsend.at[src, p], frecv.at[e, d], igs.at[src, p], fr.at[e, d], (behind, src, p)
        )

    def rows_in(src, p):
        return remote(
            igsend.at[src, p], frecv.at[src, p], igs.at[src, p], fr.at[src, p], (behind, src, p)
        )

    def score_back(src):
        return remote(ssend.at[src, d], srecv.at[e], ss.at[src], sr.at[e], (pipe, src, d))

    def score_in(src):
        return remote(ssend.at[src, d], srecv.at[src], ss.at[src], sr.at[src], (pipe, src, d))

    for r in range(1, DP):
        for i in range(2):
            scatter(r, i).start()

    lane = lax.broadcasted_iota(jnp.int32, (T, 128), 1)
    diagonal = lane == lax.broadcasted_iota(jnp.int32, (T, 128), 0)
    for c in given[2:]:
        c.wait()

    def column(row):
        spread = jnp.broadcast_to(row, (T, T))
        return jnp.sum(jnp.where(diagonal[:, :T], spread, 0), axis=1, keepdims=True)

    named = [column(routes_ref[0, k : k + 1, :]) for k in range(top)]
    weight = jnp.zeros((T, 128), F32)
    for k in range(top):
        share = column(comb_ref[0, k : k + 1, :].astype(F32))
        weight = weight + jnp.where(named[k] == lane, share, 0.0)
    wbuf[e, d] = weight
    for r in range(1, DP):
        weights_to(r).start()
    for c in given[:2]:
        c.wait()

    near = jnp.minimum(e, E - 1 - e)

    def source(i):
        half = (i + 1) // 2
        sign = jnp.where(i % 2 == 1, 1, -1) * jnp.where(2 * e < E, -1, 1)
        both_sides = e + sign * half
        one_side = jnp.where(e < E - 1 - e, e + (i - near), e - (i - near))
        return jnp.where(i <= 2 * near, both_sides, one_side)

    def arrive(i, first):
        src = e if first else source(i)

        def pass_on(p):
            for way in range(2):
                @pl.when(going(src, way))
                def _():
                    relay(src, p, way).start()

        for r in range(DP):
            if not (first and r == 0):
                relay(src, peer(r), 0).wait_recv()
            pass_on(peer(r))
            if first and r == 0:
                for c in loads:
                    c.wait()
                flipped[...] = wcat[:, : 2 * hd].T
        if first:
            for r in range(1, DP):
                weights_from(r).wait_recv()
        else:
            relay(src, DP, 0).wait_recv()
        pass_on(DP)
        return src

    def sides(src):
        blocks = xg[pl.ds(src * DP, DP)]
        return [blocks[:, i].reshape(DP * T, rows) for i in range(2)]

    def project(src):
        x, out = sides(src)
        q = jnp.concatenate(
            [
                jnp.dot(x, wcat[:, : 2 * hd], preferred_element_type=F32),
                jnp.dot(out, wcat[:, 2 * hd :], preferred_element_type=F32),
            ],
            axis=1,
        )
        qbuf[src * DP + d] = q.astype(BF16)
        for r in range(1, DP):
            partial_to(src, r).start()

    def finish(src, own):
        for r in range(1, DP):
            partial_from(src, r).wait_recv()
        s = qbuf[src * DP].astype(F32)
        for p in range(1, DP):
            s = s + qbuf[src * DP + p].astype(F32)
        w = wbuf[src].reshape(DP * T, 128)
        at = lax.broadcasted_iota(jnp.int32, (DP * T, 128), 1)
        g = jnp.sum(jnp.where(at == my_expert, w, 0.0), axis=1, keepdims=True)
        gate, up, hg = s[:, :hd], s[:, hd : 2 * hd], s[:, 2 * hd :]
        sig = jax.nn.sigmoid(gate)
        act = gate * sig
        hidden = jnp.where(g > 0.0, (act * up).astype(BF16).astype(F32), 0.0)
        hidden_grad = g * hg
        gate_grad = hidden_grad * up * sig * (1.0 + gate * (1.0 - sig))
        up_grad = hidden_grad * act
        score = jnp.sum(hidden * hg, axis=1, keepdims=True)
        ssend[src] = jnp.broadcast_to(score, (DP * T, 128)).reshape(DP, T, 128)
        both = jnp.concatenate([gate_grad, up_grad], axis=1)
        h_in[src] = both.astype(BF16)
        h_out[src] = (g * hidden).astype(BF16)
        ig = jnp.dot(
            both.astype(BF16), flipped[...], preferred_element_type=F32
        ).astype(BF16)
        igsend[src] = ig.reshape(DP, T, rows)
        for p in range(DP):
            rows_back(src, p).start()
        if own:
            srecv[src] = ssend[src, d]
        else:
            score_back(src).start()

    src = arrive(0, True)
    project(src)
    if E <= 4:
        near_by, far = range(1, min(E, 3)), range(3, E)
        planes = [arrive(i, False) for i in near_by]
        for plane in planes:
            project(plane)
        finish(src, True)
        for i in far:
            planes.append(arrive(i, False))
            project(planes[-1])
        for plane in planes:
            finish(plane, False)
    else:
        finish(src, True)

        @pl.loop(1, E)
        def _(i):
            src = arrive(i, False)
            project(src)
            finish(src, False)

    if E <= 4:
        blocks = xg[...]
        x, out = [blocks[:, i].reshape(E * DP * T, rows) for i in range(2)]
        inward = lax.dot_general(
            x, h_in[...].reshape(E * DP * T, 2 * hd), contract_first, preferred_element_type=F32
        )
        gg_ref[0] = inward[:, :hd]
        gu_ref[0] = inward[:, hd:]
        gd_ref[0] = lax.dot_general(
            out, h_out[...].reshape(E * DP * T, hd), contract_first, preferred_element_type=F32
        )
    else:
        for ref in (gg_ref, gu_ref, gd_ref):
            ref[0] = jnp.zeros((rows, hd), F32)

        @pl.loop(0, E)
        def _(j):
            x, out = sides(j)
            inward = lax.dot_general(x, h_in[j], contract_first, preferred_element_type=F32)
            gg_ref[0] = gg_ref[0] + inward[:, :hd]
            gu_ref[0] = gu_ref[0] + inward[:, hd:]
            gd_ref[0] = gd_ref[0] + lax.dot_general(
                out, h_out[j], contract_first, preferred_element_type=F32
            )

    loop(E - 1, lambda r: score_in(other(r + 1)).wait_recv())
    for k in range(top):
        out = jnp.zeros((T, 128), F32)
        for j in range(E):
            if j % slices == 0:
                per = srecv[j]
                for m in range(1, slices):
                    per = per + srecv[j + m]
                out = out + jnp.where(named[k] == j // slices, per, 0.0)
        row = jnp.sum(jnp.where(diagonal, out, 0.0), axis=0, keepdims=True)
        gc_ref[0, k : k + 1, :] = row[:, :T]

    for r in range(1, DP):
        for i in range(2):
            scatter(r, i).wait_send()
        weights_to(r).wait_send()

    def sent(i):
        src = source(i)
        for p in [peer(r) for r in range(DP)] + [DP]:
            for way in range(2):
                @pl.when(going(src, way))
                def _():
                    relay(src, p, way).wait_send()
        for p in range(DP):
            rows_back(src, p).wait_send()
        for r in range(1, DP):
            partial_to(src, r).wait_send()

    loop(E, sent)

    loop(E - 1, lambda r: score_back(other(r + 1)).wait_send())

    loop(E, lambda j: loop(DP, lambda p: rows_in(j, p).wait_recv()))
    for p in range(DP):
        if E <= 4:
            total = frecv[0, p].astype(F32)
            for j in range(1, E):
                total = total + frecv[j, p].astype(F32)
        else:
            total = lax.fori_loop(
                0, E, lambda j, t: t + frecv[j, p].astype(F32), jnp.zeros((T, rows), F32)
            )
        passed_ref[0, :, p * rows : (p + 1) * rows] = total.astype(BF16)


def write_out(*refs):
    count = len(refs) // 2
    sems = refs[-1]
    copies = [
        pltpu.make_async_copy(refs[i], refs[count + i], sems.at[i]) for i in range(count)
    ]
    for c in copies:
        c.start()
    for c in copies:
        c.wait()


def solution(mesh):
    pipes, E, DP = (mesh.shape[a] for a in ("pipe", "expert", "dp"))
    slices = min(8, E // 2)

    def body(tokens, grad_out, routes, combine, w_gate, w_up, w_down):
        T, D = tokens.shape[1:]
        top = routes.shape[2]
        rows, hd = w_gate.shape[1:]
        vmem = pl.BlockSpec(memory_space=pltpu.VMEM)
        hbm = pl.BlockSpec(memory_space=pltpu.HBM)
        dma = pltpu.SemaphoreType.DMA
        grad = jax.ShapeDtypeStruct((1, rows, hd), F32)
        shapes = (
            jax.ShapeDtypeStruct((1, T, D), BF16),
            jax.ShapeDtypeStruct((1, top, T), F32),
            grad, grad, grad,
        )
        results = pl.pallas_call(
            functools.partial(kernel, (pipes, E, DP, slices)),
            out_shape=shapes,
            in_specs=[hbm] * 7,
            out_specs=[vmem] * 5,
            scratch_shapes=[
                pltpu.VMEM((1, top, T), jnp.int32),
                pltpu.VMEM((1, top, T), BF16),
                pltpu.VMEM((E * DP, 2, T, rows), BF16),
                pltpu.VMEM((E, DP, T, 128), F32),
                pltpu.VMEM((rows, 3 * hd), BF16),
                pltpu.VMEM((2 * hd, rows), BF16),
                pltpu.VMEM((E * DP, DP * T, 3 * hd), BF16),
                pltpu.VMEM((E, DP * T, 2 * hd), BF16),
                pltpu.VMEM((E, DP * T, hd), BF16),
                pltpu.VMEM((E, DP, T, rows), BF16),
                pltpu.VMEM((E, DP, T, 128), F32),
                pltpu.VMEM((E, T, 128), F32),
                pltpu.VMEM((E, DP, T, rows), BF16),
                dma((4,)), dma((3,)), dma((DP, 2)), dma((DP,)), dma((DP,)),
                dma((E, DP + 1)), dma((2, E, DP + 1)), dma((E, DP)), dma((E, DP)),
                dma((E, DP)), dma((E,)), dma((E,)), dma((E, DP)),
            ],
            compiler_params=pltpu.CompilerParams(
                collective_id=0, has_side_effects=True, vmem_limit_bytes=48 * 2**20
            ),
        )(
            *(
                pltpu.with_memory_space_constraint(a, pltpu.HBM)
                for a in (
                    tokens, grad_out, jnp.swapaxes(routes, 1, 2), jnp.swapaxes(combine, 1, 2),
                    w_gate, w_up, w_down,
                )
            )
        )
        passed, grad_combine, *grads = pl.pallas_call(
            write_out,
            out_shape=shapes,
            in_specs=[vmem] * 5,
            out_specs=[hbm] * 5,
            scratch_shapes=[dma((5,))],
            compiler_params=pltpu.CompilerParams(vmem_limit_bytes=2 * 2**20),
        )(*results)
        return (passed, jnp.swapaxes(grad_combine, 1, 2), *grads)

    weights = P("pipe", "dp", "expert")
    mine = P("pipe", ("expert", "dp"), None)
    return jax.shard_map(
        body, mesh=mesh, in_specs=(mine,) * 4 + (weights,) * 3,
        out_specs=(mine, mine, weights, weights, weights), check_vma=False,
    )
```
